32 devices in a mesh: wide: 8 (over y, x, core), narrow: 4 (over z).
Axes of the slice: x: 2, y: 2, z: 4, core: 2. Of those that a mesh axis runs over, the one named last changes fastest.
Arguments:
- tokens: bfloat16 [32, 1024, 1024], P(('wide', 'narrow')), may hold values from -6 to 6
- lengths: int32 [32, 8], P(('wide', 'narrow')), may hold values from 1 to 256, 1024 in all within a row
- ln1_gain: bfloat16 [1024], P('narrow'), may hold values from 0.5 to 1.5
- ln1_bias: bfloat16 [1024], P('narrow'), may hold values from -2 to 2
- w_query: bfloat16 [1024, 1024], P('narrow'), may hold values from -0.1875 to 0.1875
- w_key: bfloat16 [1024, 1024], P('narrow'), may hold values from -0.1875 to 0.1875
- w_value: bfloat16 [1024, 1024], P('narrow'), may hold values from -0.1875 to 0.1875
- w_out: bfloat16 [1024, 1024], P('narrow'), may hold values from -0.75 to 0.75
- ln2_gain: bfloat16 [1024], P('narrow'), may hold values from 0.5 to 1.5
- ln2_bias: bfloat16 [1024], P('narrow'), may hold values from -2 to 2
- w_gate: bfloat16 [1024, 4096], P('narrow'), may hold values from -0.1875 to 0.1875
- w_up: bfloat16 [1024, 4096], P('narrow'), may hold values from -0.1875 to 0.1875
- w_down: bfloat16 [4096, 1024], P('narrow'), may hold values from -0.09375 to 0.09375
- cotangent: bfloat16 [32, 1024, 1024], P(('wide', 'narrow')), may hold values from -6 to 6
Outputs:
- output: bfloat16 [32, 1024, 1024], P(('wide', 'narrow'))
- input_grad: float32 [32, 1024, 1024], P(('wide', 'narrow'))
- grad_ln1_gain: float32 [1024], P('narrow')
- grad_ln1_bias: float32 [1024], P('narrow')
- grad_query: float32 [1024, 1024], P('narrow')
- grad_key: float32 [1024, 1024], P('narrow')
- grad_value: float32 [1024, 1024], P('narrow')
- grad_out: float32 [1024, 1024], P('narrow')
- grad_ln2_gain: float32 [1024], P('narrow')
- grad_ln2_bias: float32 [1024], P('narrow')
- grad_gate: float32 [1024, 4096], P('narrow')
- grad_up: float32 [1024, 4096], P('narrow')
- grad_down: float32 [4096, 1024], P('narrow')
The draws below stay inside these ranges and needn't reach their ends.
Inputs may be any that keep to these rules, and one draw needn't show every extreme that they name: Each row's 8 window lengths sum to 1024; in every row the longest window has exactly 256 tokens.
All inputs are finite; a program needn't handle non-finite values.
Results may differ from the reference program's by a relative error of at most 0.017.
Values may be sent and summed in bfloat16 or wider, within the bound.
A program may use at most 320 MiB of HBM per device.

```python
import math
import jax
import jax.numpy as jnp
import numpy as np
from jax import lax

D = 1024
FF = 4096
HEAD = 64
ROW_LEN = 1024
SEGS = 8
ROWS = 32


def level_of(stream_key, dims, shards, least, top_value):
    def one(dim, parts):
        steps = jax.random.uniform(jax.random.fold_in(jax.random.fold_in(stream_key, 6), dim), (parts,), jnp.float32, least / len(shards), top_value / len(shards))
        return jnp.repeat(jnp.exp(steps), dims[dim] // parts).reshape((-1,) + (1,) * (len(dims) - dim - 1))

    gain = one(*shards[0])
    for cut in shards[1:]:
        gain = gain * one(*cut)
    return gain


def split_up(amount, total, reach, lean):
    weights = [(1 << 20) // math.isqrt(grade ** lean) + 1 for grade in range(2, amount + 1)]
    rest, counts = total - reach - (amount - 1), [1] * (amount - 1)
    while rest > 0:
        movable = [i for i in range(amount - 1) if counts[i] < reach]
        mass, remaining = sum([weights[i] for i in movable]), rest
        for i in movable:
            extra = min(reach - counts[i], max(1, remaining * weights[i] // mass), rest)
            counts[i] = counts[i] + extra
            rest = rest - extra
    return np.array([reach] + counts)


def ragged(key, amount, total, bound, skew):
    if amount == 2:
        one = jax.random.randint(key, (), max(1, total - bound), min(bound, total - 1) + 1)
        return jnp.stack([one, total - one])
    sizes = jnp.asarray(split_up(amount, total, bound, skew), jnp.int32)
    pairs = (amount - 1) // 2
    donor, sink = sizes[1:1 + 2 * pairs:2], sizes[2:2 + 2 * pairs:2]
    room = jnp.minimum(donor - 1, bound - sink)
    shifted = jax.random.randint(jax.random.fold_in(key, 1), (pairs,), 0, 1 << 20) % (room + 1)
    sizes = sizes.at[1:1 + 2 * pairs:2].set(donor - shifted).at[2:2 + 2 * pairs:2].set(sink + shifted)
    return sizes[jax.random.permutation(jax.random.fold_in(key, 2), amount)]


def centred(rng, shape, width, reach, split=(), kind=jnp.bfloat16):
    drawn = width * jax.random.normal(rng, shape, jnp.float32)
    if split:
        drawn = drawn * level_of(rng, shape, split, -0.22, 0.18)
    return jnp.clip(drawn, -reach, reach).astype(kind)


def setup_inputs(seed: int = 0) -> dict:
    key_of = jax.random.split(jax.random.key(seed), 15)
    return {
        "tokens": centred(key_of[0], (ROWS, ROW_LEN, D), 1.0, 6.0, ((0, 32),)),
        "lengths": jax.vmap(lambda own: ragged(own, SEGS, ROW_LEN, ROW_LEN // 4, 1))(jax.random.split(key_of[1], ROWS)).reshape((ROWS, SEGS)).astype(jnp.int32),
        "ln1_gain": jnp.clip(1.0 + 0.1 * jax.random.normal(key_of[2], (D,), jnp.float32), 0.5, 1.5).astype(jnp.bfloat16),
        "ln1_bias": centred(key_of[3], (D,), 0.3, 2.0, ((0, 4),)),
        "w_query": centred(key_of[4], (D, D), D ** -0.5, 0.1875, ((0, 4),)),
        "w_key": centred(key_of[5], (D, D), D ** -0.5, 0.1875, ((0, 4),)),
        "w_value": centred(key_of[6], (D, D), D ** -0.5, 0.1875, ((0, 4),)),
        "w_out": centred(key_of[7], (D, D), (D // 16) ** -0.5, 0.75, ((0, 4),)),
        "ln2_gain": jnp.clip(1.0 + 0.1 * jax.random.normal(key_of[8], (D,), jnp.float32), 0.5, 1.5).astype(jnp.bfloat16),
        "ln2_bias": centred(key_of[9], (D,), 0.3, 2.0, ((0, 4),)),
        "w_gate": centred(key_of[10], (D, FF), D ** -0.5, 0.1875, ((0, 4),)),
        "w_up": centred(key_of[11], (D, FF), D ** -0.5, 0.1875, ((0, 4),)),
        "w_down": centred(key_of[12], (FF, D), FF ** -0.5, 0.09375, ((0, 4),)),
        "cotangent": centred(key_of[13], (ROWS, ROW_LEN, D), 1.0, 6.0, ((0, 32),)),
    }


epsilon = 1e-05
rotary_base = 10000.0
masked_score = -1e+30

@jax.custom_vjp
def low(v):
    return lax.optimization_barrier(v.astype(jnp.bfloat16)).astype(jnp.float32)

@jax.custom_vjp
def low_back(v):
    return v

def low_keep(v):
    return (low(v), None)

def low_pass(kept, grad):
    return (grad,)

def back_keep(v):
    return (v, None)

def back_low(kept, grad):
    return (low(grad),)
low.defvjp(low_keep, low_pass)
low_back.defvjp(back_keep, back_low)

def segments_positions(lengths, row_len):
    ends = jnp.cumsum(lengths, axis=-1).astype(jnp.int32)
    starts = ends - lengths
    places = jnp.arange(row_len, dtype=jnp.int32)
    inside = (places[None, :, None] >= starts[:, None, :]) & (places[None, :, None] < ends[:, None, :])
    numbers = jnp.arange(lengths.shape[-1], dtype=jnp.int32)
    segment = lax.optimization_barrier(jnp.sum(jnp.where(inside, numbers[None, None, :], 0), axis=-1)).astype(jnp.int32)
    offset = lax.optimization_barrier(jnp.sum(jnp.where(inside, starts[:, None, :], 0), axis=-1)).astype(jnp.int32)
    return (segment, places[None, :] - offset)

def rotary_tables(position, head_size):
    half_size = head_size // 2
    exponent = jnp.arange(half_size, dtype=jnp.float32) * (-2.0 / head_size)
    inverse = jnp.power(jnp.float32(rotary_base), exponent)
    angles = position.astype(jnp.float32)[..., None] * inverse
    angles = jnp.concatenate([angles, angles], axis=-1)
    return (jnp.cos(angles)[..., None, :], jnp.sin(angles)[..., None, :])

def turn(source, cos_table, sin_table):
    half_size = source.shape[-1] // 2
    rotated = jnp.concatenate([-source[..., half_size:], source[..., :half_size]], axis=-1)
    return source * cos_table + rotated * sin_table

def normalize(source):
    center = source - lax.optimization_barrier(jnp.mean(source, axis=-1, keepdims=True))
    inverse_std = lax.rsqrt(lax.optimization_barrier(jnp.mean(center * center, axis=-1, keepdims=True)) + epsilon)
    return center * inverse_std

def matmul(left, right):
    return jnp.dot(left, right, precision=lax.Precision.HIGHEST)

def row_forward(source, segment, cos_table, sin_table, params):
    gain_one, bias_one, query_full, key_full, value_full, out_full, gain_two, bias_two, gate_full, up_full, down_full = params
    length = source.shape[0]
    features = source.shape[1]
    heads_count = features // HEAD
    head_shape = (length, heads_count, HEAD)
    normed_one = low(normalize(source) * gain_one + bias_one)
    queries = low_back(matmul(normed_one, query_full))
    keys_pre = low_back(matmul(normed_one, key_full))
    values = low(low_back(matmul(normed_one, value_full))).reshape(head_shape)
    queries_rot = low(turn(queries.reshape(head_shape), cos_table, sin_table))
    keys_rot = low(turn(keys_pre.reshape(head_shape), cos_table, sin_table))
    scores = jnp.einsum('qhe,khe->hqk', queries_rot, keys_rot, precision=lax.Precision.HIGHEST)
    scores = low_back(scores * (1.0 / math.sqrt(HEAD)))
    same_window = segment[:, None] == segment[None, :]
    scores = jnp.where(same_window[None], scores, masked_score)
    highest = lax.optimization_barrier(jnp.max(scores, axis=-1, keepdims=True))
    raised = jnp.exp(scores - highest)
    probability = raised / lax.optimization_barrier(jnp.sum(raised, axis=-1, keepdims=True))
    attended = jnp.einsum('hqk,khe->qhe', low(probability), values, precision=lax.Precision.HIGHEST)
    attended = low(low_back(attended.reshape(length, features)))
    mixed = source + low_back(matmul(attended, out_full))
    normed_two = low(normalize(mixed) * gain_two + bias_two)
    gate_pre = low_back(matmul(normed_two, gate_full))
    up_pre = low_back(matmul(normed_two, up_full))
    hidden = low(gate_pre * jax.nn.sigmoid(gate_pre) * up_pre)
    return mixed + low_back(matmul(hidden, down_full))

def reference(tokens, lengths, ln1_gain, ln1_bias, w_query, w_key, w_value, w_out, ln2_gain, ln2_bias, w_gate, w_up, w_down, cotangent):
    segment, position = segments_positions(lengths, tokens.shape[1])
    cos_table, sin_table = rotary_tables(position, HEAD)
    params = tuple((weight.astype(jnp.float32) for weight in (ln1_gain, ln1_bias, w_query, w_key, w_value, w_out, ln2_gain, ln2_bias, w_gate, w_up, w_down)))

    def per_row(totals, items):
        source, row_segment, row_cos, row_sin, row_grad = items

        def forward(inputs, weights):
            return row_forward(inputs, row_segment, row_cos, row_sin, weights)
        result, pullback = jax.vjp(forward, source.astype(jnp.float32), params)
        grad_input, weight_grads = pullback(row_grad.astype(jnp.float32))
        totals = jax.tree.map(lambda summed, increment: summed + increment, totals, weight_grads)
        return (totals, (result.astype(jnp.bfloat16), grad_input))
    start_totals = tuple((jnp.zeros_like(weight) for weight in params))
    totals, (output, input_grad) = lax.scan(per_row, start_totals, (tokens, segment, cos_table, sin_table, cotangent))
    return (output, input_grad) + tuple(totals)
```

```python
import math

import jax
import jax.numpy as jnp
from jax import lax
from jax.sharding import PartitionSpec as P

HEAD = 64


epsilon = 1e-05
rotary_base = 10000.0
masked_score = -1e30


def segments_positions(lengths, row_len):
    order = jnp.arange(lengths.shape[-1], dtype=jnp.int32)
    before = order[:, None] <= order[None, :]
    ends = jnp.sum(jnp.where(before[None], lengths[:, :, None], 0), axis=1)
    starts = ends - lengths
    places = jnp.arange(row_len, dtype=jnp.int32)
    inside = (places[None, :, None] >= starts[:, None, :]) & (
        places[None, :, None] < ends[:, None, :]
    )
    numbers = jnp.arange(lengths.shape[-1], dtype=jnp.int32)
    segment = jnp.sum(jnp.where(inside, numbers[None, None, :], 0), axis=-1)
    offset = jnp.sum(jnp.where(inside, starts[:, None, :], 0), axis=-1)
    return (segment, places[None, :] - offset)


def rotary_tables(position, head_size):
    half_size = head_size // 2
    exponent = jnp.arange(half_size, dtype=jnp.float32) * (-2.0 / head_size)
    inverse = jnp.power(jnp.float32(rotary_base), exponent)
    angles = position.astype(jnp.float32)[..., None] * inverse
    angles = jnp.concatenate([angles, angles], axis=-1)
    return (jnp.cos(angles)[..., None, :], jnp.sin(angles)[..., None, :])


def turn(source, cos_table, sin_table):
    half_size = source.shape[-1] // 2
    rotated = jnp.concatenate([-source[..., half_size:], source[..., :half_size]], axis=-1)
    return source * cos_table + rotated * sin_table


def unturn(gradient, cos_table, sin_table):
    half_size = gradient.shape[-1] // 2
    scaled = gradient * sin_table
    back_part = jnp.concatenate([scaled[..., half_size:], -scaled[..., :half_size]], axis=-1)
    return gradient * cos_table + back_part


def normalize(source):
    center = source - jnp.mean(source, axis=-1, keepdims=True)
    inverse_std = lax.rsqrt(jnp.mean(center * center, axis=-1, keepdims=True) + epsilon)
    return (center * inverse_std, inverse_std)


def norm_back(grad_normed, normed_hat, inverse_std, gain_full):
    scaled = grad_normed * gain_full
    first_mean = jnp.mean(scaled, axis=-1, keepdims=True)
    second_mean = jnp.mean(scaled * normed_hat, axis=-1, keepdims=True)
    return inverse_std * (scaled - first_mean - normed_hat * second_mean)


def masked_scores(query_block, segment_block, keys_row, segment_row):
    scores = jnp.einsum("qhe,khe->hqk", query_block, keys_row, preferred_element_type=jnp.float32)
    scores = scores * (1.0 / math.sqrt(query_block.shape[-1]))
    same_window = segment_block[:, None] == segment_row[None, :]
    return jnp.where(same_window[None], scores, masked_score)


def split_blocks(row_array):
    length = row_array.shape[0]
    block_rows = min(512, length)
    return row_array.reshape((length // block_rows, block_rows) + row_array.shape[1:])


def attend_row(row_items):
    queries_row, keys_row, values_row, segment_row = row_items

    def one_block(block_items):
        query_block, segment_block = block_items
        scores = masked_scores(query_block, segment_block, keys_row, segment_row)
        highest = jnp.max(scores, axis=-1, keepdims=True)
        raised = jnp.exp(scores - highest)
        summed = jnp.sum(raised, axis=-1, keepdims=True)
        weights_low = (raised / summed).astype(jnp.bfloat16)
        result = jnp.einsum(
            "hqk,khe->qhe", weights_low, values_row, preferred_element_type=jnp.float32
        )
        return (result, (highest + jnp.log(summed))[..., 0])

    results, logsums = lax.map(one_block, (split_blocks(queries_row), split_blocks(segment_row)))
    return (results.reshape(queries_row.shape), logsums)


def attend_row_back(row_items):
    queries_row, keys_row, values_row, segment_row, grad_row, logsum_row = row_items
    score_scale = 1.0 / math.sqrt(queries_row.shape[-1])

    def one_block(carry, block_items):
        grad_keys_acc, grad_values_acc = carry
        query_block, segment_block, grad_block, logsum_block = block_items
        scores = masked_scores(query_block, segment_block, keys_row, segment_row)
        probability = jnp.exp(scores - logsum_block[..., None])
        grad_probs = jnp.einsum(
            "qhe,khe->hqk", grad_block, values_row, preferred_element_type=jnp.float32
        )
        row_dot = jnp.sum(probability * grad_probs, axis=-1, keepdims=True)
        grad_scores = (probability * (grad_probs - row_dot)).astype(jnp.bfloat16)
        grad_query_block = (
            jnp.einsum("hqk,khe->qhe", grad_scores, keys_row, preferred_element_type=jnp.float32)
            * score_scale
        )
        grad_keys_acc = (
            grad_keys_acc
            + jnp.einsum(
                "hqk,qhe->khe", grad_scores, query_block, preferred_element_type=jnp.float32
            )
            * score_scale
        )
        grad_values_acc = grad_values_acc + jnp.einsum(
            "hqk,qhe->khe",
            probability.astype(jnp.bfloat16),
            grad_block,
            preferred_element_type=jnp.float32,
        )
        return ((grad_keys_acc, grad_values_acc), grad_query_block)

    zero_grads = jnp.zeros(keys_row.shape, jnp.float32)
    block_items = (
        split_blocks(queries_row),
        split_blocks(segment_row),
        split_blocks(grad_row),
        logsum_row,
    )
    (grad_keys_row, grad_values_row), grad_queries_blocks = lax.scan(
        one_block, (zero_grads, zero_grads), block_items
    )
    return (grad_queries_blocks.reshape(queries_row.shape), grad_keys_row, grad_values_row)


def shards(
    tokens,
    lengths,
    ln1_gain,
    ln1_bias,
    w_query,
    w_key,
    w_value,
    w_out,
    ln2_gain,
    ln2_bias,
    w_gate,
    w_up,
    w_down,
    cotangent,
):
    rows_here, row_len, features = tokens.shape
    heads_count = features // HEAD
    head_shape = (rows_here, row_len, heads_count, HEAD)
    wide_place = lax.axis_index("wide")
    wide_size = lax.axis_size("wide")

    def gather_whole(shard):
        share = shard.shape[0] // wide_size
        piece = lax.dynamic_slice_in_dim(shard, wide_place * share, share, axis=0)
        return lax.all_gather(piece, ("narrow", "wide"), axis=0, tiled=True)

    vectors = lax.all_gather(
        jnp.stack([ln1_gain, ln1_bias, ln2_gain, ln2_bias]), "narrow", axis=1, tiled=True
    )
    gain_one, bias_one, gain_two, bias_two = vectors[0], vectors[1], vectors[2], vectors[3]
    attn_full = gather_whole(jnp.concatenate([w_query, w_key, w_value, w_out], axis=1))
    query_full, key_full, value_full, out_full = jnp.split(attn_full, 4, axis=1)
    gate_full, up_full = jnp.split(gather_whole(jnp.concatenate([w_gate, w_up], axis=1)), 2, axis=1)
    down_full = gather_whole(w_down)
    segment, position = segments_positions(lengths, row_len)
    cos_table, sin_table = rotary_tables(position, HEAD)
    tokens_flat = tokens.reshape(rows_here * row_len, features).astype(jnp.float32)
    hat_one, inverse_one = normalize(tokens_flat)
    normed_one = (hat_one * gain_one.astype(jnp.float32) + bias_one.astype(jnp.float32)).astype(
        jnp.bfloat16
    )
    queries_pre = jnp.dot(normed_one, query_full, preferred_element_type=jnp.float32).reshape(
        head_shape
    )
    keys_pre = jnp.dot(normed_one, key_full, preferred_element_type=jnp.float32).reshape(head_shape)
    queries_rot = turn(queries_pre, cos_table, sin_table).astype(jnp.bfloat16)
    keys_rot = turn(keys_pre, cos_table, sin_table).astype(jnp.bfloat16)
    values_low = (
        jnp.dot(normed_one, value_full, preferred_element_type=jnp.float32)
        .astype(jnp.bfloat16)
        .reshape(head_shape)
    )
    attended, logsum_rows = lax.map(attend_row, (queries_rot, keys_rot, values_low, segment))
    attended_low = attended.reshape(rows_here * row_len, features).astype(jnp.bfloat16)
    mixed = tokens_flat + jnp.dot(attended_low, out_full, preferred_element_type=jnp.float32)
    hat_two, inverse_two = normalize(mixed)
    normed_two = (hat_two * gain_two.astype(jnp.float32) + bias_two.astype(jnp.float32)).astype(
        jnp.bfloat16
    )
    gate_pre = jnp.dot(normed_two, gate_full, preferred_element_type=jnp.float32)
    up_pre = jnp.dot(normed_two, up_full, preferred_element_type=jnp.float32)
    sigmoid_gate = jax.nn.sigmoid(gate_pre)
    silu_gate = gate_pre * sigmoid_gate
    hidden = (silu_gate * up_pre).astype(jnp.bfloat16)
    final = mixed + jnp.dot(hidden, down_full, preferred_element_type=jnp.float32)
    output = final.astype(jnp.bfloat16).reshape(tokens.shape)
    cotangent_flat = cotangent.reshape(rows_here * row_len, features)
    grad_down = jnp.einsum("tf,td->fd", hidden, cotangent_flat, preferred_element_type=jnp.float32)
    grad_hidden = jnp.einsum(
        "td,fd->tf", cotangent_flat, down_full, preferred_element_type=jnp.float32
    )
    grad_gate_pre = (
        grad_hidden * up_pre * sigmoid_gate * (1.0 + gate_pre * (1.0 - sigmoid_gate))
    ).astype(jnp.bfloat16)
    grad_up_pre = (grad_hidden * silu_gate).astype(jnp.bfloat16)
    grad_gate = jnp.einsum(
        "td,tf->df", normed_two, grad_gate_pre, preferred_element_type=jnp.float32
    )
    grad_up = jnp.einsum("td,tf->df", normed_two, grad_up_pre, preferred_element_type=jnp.float32)
    grad_normed_two = jnp.einsum(
        "tf,df->td", grad_gate_pre, gate_full, preferred_element_type=jnp.float32
    )
    grad_normed_two = grad_normed_two + jnp.einsum(
        "tf,df->td", grad_up_pre, up_full, preferred_element_type=jnp.float32
    )
    grad_gain_two = jnp.sum(grad_normed_two * hat_two, axis=0)
    grad_bias_two = jnp.sum(grad_normed_two, axis=0)
    grad_mixed = cotangent_flat.astype(jnp.float32) + norm_back(
        grad_normed_two, hat_two, inverse_two, gain_two.astype(jnp.float32)
    )

    def sum_shards(grad):
        piece = lax.psum_scatter(
            grad.astype(jnp.bfloat16), ("narrow", "wide"), scatter_dimension=0, tiled=True
        )
        return lax.all_gather(piece, "wide", axis=0, tiled=True).astype(jnp.float32)

    grad_down_sum = sum_shards(grad_down)
    grad_gate_sum, grad_up_sum = jnp.split(
        sum_shards(jnp.concatenate([grad_gate, grad_up], axis=1)), 2, axis=1
    )
    grad_res = grad_mixed.astype(jnp.bfloat16)
    grad_out = jnp.einsum("td,te->de", attended_low, grad_res, preferred_element_type=jnp.float32)
    grad_attended = (
        jnp.einsum("te,de->td", grad_res, out_full, preferred_element_type=jnp.float32)
        .astype(jnp.bfloat16)
        .reshape(head_shape)
    )
    grad_queries_rot, grad_keys_rot, grad_values = lax.map(
        attend_row_back, (queries_rot, keys_rot, values_low, segment, grad_attended, logsum_rows)
    )
    flat_shape = (rows_here * row_len, features)
    grad_queries = (
        unturn(grad_queries_rot, cos_table, sin_table).astype(jnp.bfloat16).reshape(flat_shape)
    )
    grad_keys = unturn(grad_keys_rot, cos_table, sin_table).astype(jnp.bfloat16).reshape(flat_shape)
    grad_values_low = grad_values.astype(jnp.bfloat16).reshape(flat_shape)
    grad_query = jnp.einsum(
        "td,te->de", normed_one, grad_queries, preferred_element_type=jnp.float32
    )
    grad_key = jnp.einsum("td,te->de", normed_one, grad_keys, preferred_element_type=jnp.float32)
    grad_value = jnp.einsum(
        "td,te->de", normed_one, grad_values_low, preferred_element_type=jnp.float32
    )
    grad_normed_one = jnp.einsum(
        "te,de->td", grad_queries, query_full, preferred_element_type=jnp.float32
    )
    grad_normed_one = grad_normed_one + jnp.einsum(
        "te,de->td", grad_keys, key_full, preferred_element_type=jnp.float32
    )
    grad_normed_one = grad_normed_one + jnp.einsum(
        "te,de->td", grad_values_low, value_full, preferred_element_type=jnp.float32
    )
    grad_gain_one = jnp.sum(grad_normed_one * hat_one, axis=0)
    grad_bias_one = jnp.sum(grad_normed_one, axis=0)
    input_grad = grad_mixed + norm_back(
        grad_normed_one, hat_one, inverse_one, gain_one.astype(jnp.float32)
    )
    attn_sums = jnp.split(
        sum_shards(jnp.concatenate([grad_query, grad_key, grad_value, grad_out], axis=1)), 4, axis=1
    )
    vector_sums = lax.psum(
        jnp.stack([grad_gain_one, grad_bias_one, grad_gain_two, grad_bias_two]), ("wide", "narrow")
    )
    mine = lax.dynamic_slice_in_dim(
        vector_sums, lax.axis_index("narrow") * ln1_gain.shape[0], ln1_gain.shape[0], axis=1
    )
    return (
        output,
        input_grad.reshape(tokens.shape),
        mine[0],
        mine[1],
        *attn_sums,
        mine[2],
        mine[3],
        grad_gate_sum,
        grad_up_sum,
        grad_down_sum,
    )


def solution(mesh):
    placed = (
        P(("wide", "narrow"), None, None),
        P(("wide", "narrow"), None),
        P("narrow"),
        P("narrow"),
        P("narrow", None),
        P("narrow", None),
        P("narrow", None),
        P("narrow", None),
        P("narrow"),
        P("narrow"),
        P("narrow", None),
        P("narrow", None),
        P("narrow", None),
        P(("wide", "narrow"), None, None),
    )
    return jax.shard_map(
        shards,
        mesh=mesh,
        in_specs=placed,
        out_specs=(
            P(("wide", "narrow"), None, None),
            P(("wide", "narrow"), None, None),
            P("narrow"),
            P("narrow"),
            P("narrow", None),
            P("narrow", None),
            P("narrow", None),
            P("narrow", None),
            P("narrow"),
            P("narrow"),
            P("narrow", None),
            P("narrow", None),
            P("narrow", None),
        ),
        check_vma=False,
    )
```

```python
import functools
import math

import jax
import jax.numpy as jnp
import numpy as np
from jax import lax
from jax.experimental import pallas as pl
from jax.experimental.pallas import tpu as pltpu
from jax.sharding import PartitionSpec as P

F32 = jnp.float32
BF = jnp.bfloat16
HEAD = 64
BLK = 256
LOG2E = 1.4426950408889634
EPS = 1e-5
ROTARY_BASE = 10000.0
ANY = pl.BlockSpec(memory_space=pl.ANY)
MIB = 1024 * 1024
ZN = 4


def nn(a, b):
    return lax.dot_general(a, b, (((1,), (0,)), ((), ())), preferred_element_type=F32)


def nt(a, b):
    return lax.dot_general(a, b, (((1,), (1,)), ((), ())), preferred_element_type=F32)


def tn(a, b):
    return lax.dot_general(a, b, (((0,), (0,)), ((), ())), preferred_element_type=F32)


def lanes(shape):
    return lax.broadcasted_iota(jnp.int32, shape, len(shape) - 1)


def hat_of(x):
    center = x - jnp.mean(x, axis=-1, keepdims=True)
    rstd = lax.rsqrt(jnp.mean(center * center, axis=-1, keepdims=True) + EPS)
    return center * rstd, rstd


def norm_back(grad, hat, rstd, gain):
    scaled = grad * gain
    first = jnp.mean(scaled, axis=-1, keepdims=True)
    second = jnp.mean(scaled * hat, axis=-1, keepdims=True)
    return rstd * (scaled - first - hat * second)


def halves(u):
    first = lax.rem(lanes(u.shape), HEAD) < HEAD // 2
    ahead = pltpu.roll(u, u.shape[-1] - HEAD // 2, axis=u.ndim - 1)
    behind = pltpu.roll(u, HEAD // 2, axis=u.ndim - 1)
    return jnp.where(first, ahead, behind)


def turn(u, cos, sin_signed):
    return u * cos + halves(u) * sin_signed


def unturn(g, cos, sin_signed):
    return g * cos - halves(g) * sin_signed


def copies(pairs, sems):
    made = [pltpu.make_async_copy(a, b, sems.at[i]) for i, (a, b) in enumerate(pairs)]
    for one in made:
        one.start()
    return made


def split_three(v):
    top = v.astype(BF).astype(F32)
    rest = v - top
    mid = rest.astype(BF).astype(F32)
    return top, mid, rest - mid


MESH_ID = pl.DeviceIdType.MESH


def place():
    w, z = lax.axis_index("wide"), lax.axis_index("narrow")
    c, a, b = lax.rem(w, 2), lax.rem(w // 2, 2), lax.rem(w // 4, 2)
    return dict(w=w, z=z, c=c, a=a, b=b, wc=w + 1 - 2 * c, wx=w + 2 - 4 * a, wy=w + 4 - 8 * b)


def around(me, k):
    return lax.rem(me["z"] + k + ZN, ZN)


def remote(src, dst, ssem, rsem, w, z):
    return pltpu.make_async_remote_copy(
        src_ref=src, dst_ref=dst, send_sem=ssem, recv_sem=rsem, device_id=(w, z), device_id_type=MESH_ID
    )


def meet(me):
    barrier = pltpu.get_barrier_semaphore()
    others = [(me["wc"], me["z"]), (me["wx"], me["z"]), (me["wy"], me["z"])]
    others += [(me["w"], around(me, k)) for k in range(1, ZN)]
    for other in others:
        pl.semaphore_signal(barrier, inc=1, device_id=other, device_id_type=MESH_ID)
    pl.semaphore_wait(barrier, len(others))


def part(start, size):
    return pl.ds(pl.multiple_of(start, size), size)


LEFT, RIGHT = pl.ds(0, 512), pl.ds(512, 512)


class Gather:
    def __init__(self, me, own, dst, ssem, rsem):
        self.me, self.own, self.dst, self.ssem, self.rsem = me, own, dst, ssem, rsem
        c, a, b = me["c"], me["a"], me["b"]
        self.mine = part(c * 128 + a * 64 + b * 32, 32)
        self.from_x = part(c * 128 + (1 - a) * 64 + b * 32, 32)
        self.from_y = part(c * 128 + a * 64 + (1 - b) * 32, 32)
        self.core_half = part(c * 128, 128)

    def along(self, p, k, rows, cols, at, w, z, owner):
        ref = self.dst.at[p, owner, rows, cols]
        return remote(ref, ref, self.ssem.at[p, at + k - 1], self.rsem.at[p, at + k - 1], w, z)

    def z_copy(self, p, k):
        me = self.me
        src, dst = self.own.at[p, self.mine], self.dst.at[p, me["z"], self.mine]
        return remote(src, dst, self.ssem.at[p, k - 1], self.rsem.at[p, k - 1], me["w"], around(me, k))

    def x_copy(self, p, k):
        return self.along(p, k, self.mine, pl.ds(0, 1024), 3, self.me["wx"], self.me["z"], around(self.me, -k))

    def y_copy(self, p, k):
        return self.along(p, k, self.mine, pl.ds(0, 1024), 6, self.me["wy"], self.me["z"], around(self.me, -k))

    def xy_copy(self, p, k):
        return self.along(p, k, self.from_y, LEFT, 9, self.me["wx"], self.me["z"], around(self.me, -k))

    def yx_copy(self, p, k):
        return self.along(p, k, self.from_x, RIGHT, 12, self.me["wy"], self.me["z"], around(self.me, -k))

    def core_copy(self, p, k):
        return self.along(p, k, self.core_half, pl.ds(0, 1024), 15, self.me["wc"], self.me["z"], around(self.me, -k))

    def start_z(self, p):
        for k in range(1, ZN):
            self.z_copy(p, k).start()

    def stage_one(self, p):
        for k in range(1, ZN):
            self.z_copy(p, k).wait_recv()
            self.x_copy(p, k).start()
            self.y_copy(p, k).start()

    def stage_two(self, p):
        for k in range(1, ZN):
            self.y_copy(p, k).wait_recv()
            self.xy_copy(p, k).start()
            self.x_copy(p, k).wait_recv()
            self.yx_copy(p, k).start()

    def stage_core(self, p):
        for k in range(1, ZN):
            self.xy_copy(p, k).wait_recv()
            self.yx_copy(p, k).wait_recv()
            self.core_copy(p, k).start()

    def finish(self, p):
        for k in range(1, ZN):
            self.core_copy(p, k).wait_recv()
        for k in range(1, ZN):
            for copy in (self.z_copy, self.x_copy, self.y_copy, self.xy_copy, self.yx_copy, self.core_copy):
                copy(p, k).wait_send()


def add_up(*parts):
    total = parts[0].astype(F32)
    for one in parts[1:]:
        total = total + one.astype(F32)
    return total.astype(BF)


class Reduce:
    SCRATCH = [
        ((2, 4, 128, 1024), "r0"), ((4, 128, 1024), "s0"), ((2, 2, 4, 64, 512), "r1"), ((2, 4, 64, 512), "s1"),
        ((2, 2, 4, 32, 512), "r2"), ((4, 2, 32, 512), "s2"), ((2, 3, 2, 32, 512), "r3"), ((2, 2, 32, 512), "f"),
    ]

    def __init__(self, me, G, fin, bufs, ssem, rsem, lsem):
        self.me, self.G, self.fin, self.ssem, self.rsem, self.lsem = me, G, fin, ssem, rsem, lsem
        for (_shape, name), ref in zip(self.SCRATCH, bufs):
            setattr(self, name, ref)

    def to(self, p, i, src, dst, w, z=None):
        z = self.me["z"] if z is None else z
        slot = lax.rem(p, 2)
        return remote(src, dst, self.ssem.at[slot, i], self.rsem.at[slot, i], w, z)

    def copies(self, s, p):
        me = self.me
        a, b, c, slot = me["a"], me["b"], me["c"], lax.rem(p, 2)
        every = pl.ds(0, ZN)
        if s == 0:
            return [self.to(p, 0, self.G.at[slot, every, part((1 - c) * 128, 128)], self.r0.at[slot], me["wc"])]
        if s == 1:
            return [
                self.to(p, 1, self.s0.at[every, part((1 - a) * 64, 64), LEFT], self.r1.at[slot, 0], me["wx"]),
                self.to(p, 2, self.s0.at[every, part((1 - b) * 64, 64), RIGHT], self.r1.at[slot, 1], me["wy"]),
            ]
        if s == 2:
            return [
                self.to(p, 3, self.s1.at[0, every, part((1 - b) * 32, 32)], self.r2.at[slot, 0], me["wy"]),
                self.to(p, 4, self.s1.at[1, every, part((1 - a) * 32, 32)], self.r2.at[slot, 1], me["wx"]),
            ]
        if s == 3:
            return [
                self.to(p, 4 + k, self.s2.at[around(me, k)], self.r3.at[slot, k - 1], me["w"], around(me, k))
                for k in range(1, ZN)
            ]
        left = (part(c * 128 + a * 64 + b * 32, 32), LEFT)
        right = (part(c * 128 + b * 64 + a * 32, 32), RIGHT)
        if s == 4:
            return [
                self.to(p, 8, self.f.at[slot, 0], self.fin.at[p, left[0], left[1]], me["wy"]),
                self.to(p, 9, self.f.at[slot, 1], self.fin.at[p, right[0], right[1]], me["wx"]),
                pltpu.make_async_copy(self.f.at[slot, 0], self.fin.at[p, left[0], left[1]], self.lsem.at[slot, 0]),
                pltpu.make_async_copy(self.f.at[slot, 1], self.fin.at[p, right[0], right[1]], self.lsem.at[slot, 1]),
            ]
        if s == 5:
            left = self.fin.at[p, part(c * 128 + a * 64, 64), LEFT]
            right = self.fin.at[p, part(c * 128 + b * 64, 64), RIGHT]
            return [self.to(p, 10, left, left, me["wx"]), self.to(p, 11, right, right, me["wy"])]
        half = self.fin.at[p, part(c * 128, 128)]
        return [self.to(p, 12, half, half, me["wc"])]

    def start(self, s, p):
        for copy in self.copies(s, p):
            copy.start()

    def take(self, s, p):
        for copy in self.copies(s, p):
            copy.wait()
        me = self.me
        a, b, c, z, slot = me["a"], me["b"], me["c"], me["z"], lax.rem(p, 2)
        if s == 0:
            for k in range(ZN):
                self.s0[k] = add_up(self.G[slot, k, part(c * 128, 128), :], self.r0[slot, k])
        if s == 1:
            self.s1[0] = add_up(self.s0[:, part(a * 64, 64), 0:512], self.r1[slot, 0])
            self.s1[1] = add_up(self.s0[:, part(b * 64, 64), 512:1024], self.r1[slot, 1])
        if s == 2:
            self.s2[:, 0] = add_up(self.s1[0, :, part(b * 32, 32), :], self.r2[slot, 0])
            self.s2[:, 1] = add_up(self.s1[1, :, part(a * 32, 32), :], self.r2[slot, 1])
        if s == 3:
            self.f[slot] = add_up(self.s2[z], self.r3[slot, 0], self.r3[slot, 1], self.r3[slot, 2])

    def advance(self, s, p):
        self.take(s, p)
        if s < 6:
            self.start(s + 1, p)

    def slot(self, t, low, high):
        for s in range(6, -1, -1):
            p = t - 1 - s

            @pl.when((p >= low) & (p < high))
            def _due(s=s, p=p):
                self.advance(s, p)


def local_feed(gate, up, own, sems, i):
    at = 4 + 3 * (i // 2) + lax.rem(i, 2)
    made = []
    for j in range(ZN):
        cols = part(1024 * j + 128 * i, 128)
        made.append(pltpu.make_async_copy(gate.at[:, cols], own.at[at, :, pl.ds(128 * j, 128)], sems.at[1 + i, j]))
        to = pl.ds(512 + 128 * j, 128)
        made.append(pltpu.make_async_copy(up.at[:, cols], own.at[at, :, to], sems.at[1 + i, 4 + j]))
    return made


def local_down(down, own, sems, i):
    return pltpu.make_async_copy(down.at[part(256 * i, 256)], own.at[6 + 3 * i], sems.at[9, i])


def loop(n, body):
    def step(i, _):
        body(i)
        return 0

    lax.fori_loop(0, n, step, 0)


def starts(make):
    def body(i):
        made = make(i)
        for copy in made if isinstance(made, list) else [made]:
            copy.start()

    return body


def waits(make):
    def body(i):
        made = make(i)
        for copy in made if isinstance(made, list) else [made]:
            copy.wait()

    return body


def kernel_gather(q, k, v, o, gate, up, down, dst, own, lsem, ssem, rsem):
    me = place()
    z = me["z"]
    local = [pltpu.make_async_copy(m, own.at[i], lsem.at[0, i]) for i, m in enumerate((q, k, v, o))]
    for copy in local:
        copy.start()
    loop(8, starts(lambda i: local_feed(gate, up, own, lsem, i)))
    loop(4, starts(lambda i: local_down(down, own, lsem, i)))
    meet(me)
    g = Gather(me, own, dst, ssem, rsem)

    def put(p):
        return pltpu.make_async_copy(own.at[p], dst.at[p, z], lsem.at[10, p])

    for i, copy in enumerate(local):
        copy.wait()
        g.start_z(i)
    loop(8, waits(lambda i: local_feed(gate, up, own, lsem, i)))
    loop(4, waits(lambda i: local_down(down, own, lsem, i)))
    n = dst.shape[0]
    loop(n, starts(put))

    def slot(t, _):
        for stage, lag in ((g.finish, 4), (g.stage_core, 3), (g.stage_two, 2), (g.stage_one, 1)):
            p = t - lag

            @pl.when((p >= 0) & (p < n))
            def _due(stage=stage, p=p):
                stage(p)

        @pl.when((t >= 4) & (t < n))
        def _z():
            g.start_z(t)

        return 0

    lax.fori_loop(1, n + 4, slot, 0)
    loop(n, waits(put))


def run_gather(*shards_):
    return pl.pallas_call(
        kernel_gather,
        name="weights",
        out_shape=jax.ShapeDtypeStruct((16, ZN, 256, 1024), BF),
        in_specs=[ANY] * 7,
        out_specs=ANY,
        scratch_shapes=[
            pltpu.VMEM((16, 256, 1024), BF),
            pltpu.SemaphoreType.DMA((11, 16)), pltpu.SemaphoreType.DMA((16, 18)), pltpu.SemaphoreType.DMA((16, 18)),
        ],
        compiler_params=pltpu.CompilerParams(collective_id=0, has_side_effects=True, vmem_limit_bytes=40 * MIB),
    )(*shards_)


def kernel_reduce(Ga_h, G_h, fin, G, *rest):
    bufs, (ssem, rsem, lsem, gsem) = rest[:8], rest[8:]
    me = place()
    n = G_h.shape[0]

    def load(p):
        return pltpu.make_async_copy(G_h.at[p], G.at[lax.rem(p, 2)], gsem.at[lax.rem(p, 2)])

    def load_start(p):
        @pl.when(p < 4)
        def _attn():
            pltpu.make_async_copy(Ga_h.at[p], G.at[lax.rem(p, 2)], gsem.at[lax.rem(p, 2)]).start()

        @pl.when(p >= 4)
        def _feed():
            load(p).start()

    load_start(jnp.int32(0))
    meet(me)
    r = Reduce(me, G, fin, bufs, ssem, rsem, lsem)

    def slot(t, _):
        r.slot(t, 0, n)

        @pl.when(t < n)
        def _begin():
            load(t).wait()
            r.start(0, t)

        @pl.when(t + 1 < n)
        def _load():
            load_start(t + 1)

        return 0

    lax.fori_loop(0, n + 7, slot, 0)


def run_reduce(Ga, G):
    return pl.pallas_call(
        kernel_reduce,
        name="gradient_sums",
        out_shape=jax.ShapeDtypeStruct((G.shape[0], 256, 1024), BF),
        in_specs=[ANY, ANY],
        out_specs=ANY,
        scratch_shapes=[pltpu.VMEM((2, ZN, 256, 1024), BF)]
        + [pltpu.VMEM(shape, BF) for shape, _ in Reduce.SCRATCH]
        + [
            pltpu.SemaphoreType.DMA((2, 13)), pltpu.SemaphoreType.DMA((2, 13)), pltpu.SemaphoreType.DMA((2, 2)),
            pltpu.SemaphoreType.DMA((2,)),
        ],
        compiler_params=pltpu.CompilerParams(collective_id=1, has_side_effects=True, vmem_limit_bytes=40 * MIB),
    )(Ga, G)


def attention_forward(i, pair, qaug, kaug, vaug, att):
    T = qaug.shape[0]
    low, high = max(0, i - 1) * BLK, min(T, (i + 2) * BLK)
    rows = slice(i * BLK, (i + 1) * BLK)
    outs, tops = [], []
    for one in range(2):
        cols = pl.ds(pl.multiple_of((2 * pair + one) * 128, 128), 128)
        scores = nt(qaug[rows, cols], kaug[low:high, cols])
        top = jnp.max(scores, axis=-1, keepdims=True)
        raised = jnp.exp2(scores - top).astype(BF)
        outs.append(nn(raised, vaug[low:high, cols]))
        tops.append(top)
    lane = lanes((BLK, 128))
    left = lane < HEAD
    for one in range(2):
        cols = pl.ds(pl.multiple_of((2 * pair + one) * 128, 128), 128)
        base = HEAD if one == 0 else 0
        parts = split_three(-(tops[one] + jnp.log2(outs[one])))
        kept = qaug[rows, cols].astype(F32)
        for k, part in enumerate(parts):
            kept = jnp.where(lane == base + 8 + k, part, kept)
        qaug[rows, cols] = kept.astype(BF)
    summed = pltpu.roll(jnp.where(left, outs[1], outs[0]), HEAD, axis=1)
    att[rows, pl.ds(pl.multiple_of(pair * 128, 128), 128)] = (
        jnp.where(left, outs[0], outs[1]) / summed
    ).astype(BF)


def project_turned(n1, W, cos, sin, aug, dest, scale):
    T = n1.shape[0]

    def block(j, _):
        flat = nn(n1[...], W[:, :, part(j * 256, 256)].reshape(n1.shape[1], 256))
        left = lanes((T, 128)) < HEAD
        for p in range(2):
            u = turn(flat[:, 128 * p : 128 * p + 128], cos[...], sin[...])
            if scale != 1.0:
                u = u * scale
            extra = aug[...].astype(F32)
            at = (4 * j + 2 * p) * 128
            dest[:, pl.ds(pl.multiple_of(at, 128), 128)] = jnp.where(left, u, extra).astype(BF)
            dest[:, pl.ds(pl.multiple_of(at + 128, 128), 128)] = jnp.where(left, extra, u).astype(BF)
        return 0

    lax.fori_loop(0, n1.shape[1] // 256, block, 0)


def project_values(n1, W, dest):
    T = n1.shape[0]

    def block(j, _):
        flat = nn(n1[...], W[:, :, part(j * 256, 256)].reshape(n1.shape[1], 256))
        left = lanes((T, 128)) < HEAD
        for p in range(2):
            u = flat[:, 128 * p : 128 * p + 128]
            at = (4 * j + 2 * p) * 128
            dest[:, pl.ds(pl.multiple_of(at, 128), 128)] = jnp.where(left, u, 1.0).astype(BF)
            dest[:, pl.ds(pl.multiple_of(at + 128, 128), 128)] = jnp.where(left, 1.0, u).astype(BF)
        return 0

    lax.fori_loop(0, n1.shape[1] // 256, block, 0)


def norm_rows(source, dest, gain, bias, n=BLK):
    def block(r, _):
        rows = pl.ds(pl.multiple_of(r * n, n), n)
        hat, _unused = hat_of(source[rows, :].astype(F32))
        dest[rows, :] = (hat * gain + bias).astype(BF)
        return 0

    lax.fori_loop(0, source.shape[0] // n, block, 0)


def kernel_a(
    tok_h, vec_h, cos_h, sin_h, aq_h, ak_h, W_h,
    mixed_h, n2_h, n1_h, att_h, qaug_h, kaug_h, vaug_h,
    x, vec, cos, sin, aq, ak, W, n1, qaug, kaug, vaug, att, mixed, sems, osems,
):
    T = x.shape[0]
    first = copies(
        [(tok_h, x), (vec_h, vec), (cos_h, cos), (sin_h, sin), (aq_h, aq), (ak_h, ak)]
        + [(W_h.at[k], W.at[k]) for k in range(4)],
        sems,
    )
    first[0].wait()
    first[1].wait()
    norm_rows(x, n1, vec[0:1, :], vec[1:2, :])
    for one in first[2:7]:
        one.wait()
    project_turned(n1, W.at[0], cos, sin, aq, qaug, LOG2E / math.sqrt(HEAD))
    first[7].wait()
    project_turned(n1, W.at[1], cos, sin, ak, kaug, 1.0)
    first[8].wait()
    project_values(n1, W.at[2], vaug)
    first[9].wait()
    outs = copies([(n1, n1_h), (kaug, kaug_h), (vaug, vaug_h)], osems)

    def per_pair(pair, _):
        for i in range(T // BLK):
            attention_forward(i, pair, qaug, kaug, vaug, att)
        return 0

    lax.fori_loop(0, x.shape[1] // 128, per_pair, 0)
    more = [pltpu.make_async_copy(qaug, qaug_h, osems.at[3]), pltpu.make_async_copy(att, att_h, osems.at[4])]
    for one in more:
        one.start()
    mixed[...] = x[...].astype(F32) + nn(att[...], W[3].reshape(x.shape[1], x.shape[1]))
    last = pltpu.make_async_copy(mixed, mixed_h, osems.at[5])
    last.start()
    outs[0].wait()
    norm_rows(mixed, n1, vec[2:3, :], vec[3:4, :])
    pltpu.make_async_copy(n1, n2_h, osems.at[6]).start()
    pltpu.make_async_copy(n1, n2_h, osems.at[6]).wait()
    for one in outs[1:] + more + [last]:
        one.wait()


def run_a(tok, vec, cos, sin, aq, ak, W):
    T, D = tok.shape
    sds = jax.ShapeDtypeStruct
    return pl.pallas_call(
        kernel_a,
        name="attention_forward",
        out_shape=[
            sds((T, D), F32), sds((T, D), BF), sds((T, D), BF), sds((T, D), BF),
            sds((T, 2 * D), BF), sds((T, 2 * D), BF), sds((T, 2 * D), BF),
        ],
        in_specs=[ANY] * 7,
        out_specs=[ANY] * 7,
        scratch_shapes=[
            pltpu.VMEM((T, D), BF), pltpu.VMEM(vec.shape, F32), pltpu.VMEM((T, 128), F32), pltpu.VMEM((T, 128), F32),
            pltpu.VMEM((T, 128), BF), pltpu.VMEM((T, 128), BF), pltpu.VMEM((4, ZN, D // ZN, D), BF), pltpu.VMEM((T, D), BF),
            pltpu.VMEM((T, 2 * D), BF), pltpu.VMEM((T, 2 * D), BF), pltpu.VMEM((T, 2 * D), BF),
            pltpu.VMEM((T, D), BF), pltpu.VMEM((T, D), F32),
            pltpu.SemaphoreType.DMA((10,)), pltpu.SemaphoreType.DMA((7,)),
        ],
        compiler_params=pltpu.CompilerParams(vmem_limit_bytes=60 * MIB),
    )(tok, vec, cos, sin, aq, ak, W)


def feed_chunk(n2, cot, gate_up, down, G, Gd, hid, dgu, oacc, gacc):
    D = n2.shape[1]
    half = hid.shape[1]
    gu = nn(n2[...], gate_up[...].reshape(D, 2 * half))
    g = gu[:, :half]
    u = gu[:, half:]
    gh = nt(cot[...], down[...].reshape(half, D))
    sig = 0.5 * jnp.tanh(0.5 * g) + 0.5
    silu = g * sig
    hid[...] = (silu * u).astype(BF)
    dgu[:, :half] = (gh * u * (sig + silu * (1.0 - sig))).astype(BF)
    dgu[:, half:] = (gh * silu).astype(BF)
    oacc[...] += nn(hid[...], down[...].reshape(half, D))
    gacc[...] += nt(dgu[...], gate_up[...].reshape(D, 2 * half))
    G[...] = tn(n2[...], dgu[...]).astype(BF).reshape(G.shape)
    Gd[...] = tn(hid[...], cot[...]).astype(BF).reshape(Gd.shape)


def kernel_b(
    n2_h, cot_h, mixed_h, vec_h, W_h,
    out_h, gm_h, vecs_h, G_h,
    n2, cot, mixed, vec, oacc, gacc, W, Wd, hid, dgu, G, Gd, vecs, s, sw, sg,
):
    T = n2.shape[0]
    chunks = 8
    first = copies([(n2_h, n2), (cot_h, cot), (mixed_h, oacc), (mixed_h, mixed), (vec_h, vec)], s)

    def wcp(c):
        at, slot = 4 + 3 * (c // 2), c % 2
        half = W_h.at[at + 2, :, part(slot * 128, 128)]
        return [
            pltpu.make_async_copy(W_h.at[at + slot], W.at[slot], sw.at[slot, 0]),
            pltpu.make_async_copy(half, Wd.at[slot], sw.at[slot, 1]),
        ]

    def gcp(c):
        at, slot = 4 + 3 * (c // 2), c % 2
        half = G_h.at[at + 2, :, part(slot * 128, 128)]
        return [
            pltpu.make_async_copy(G.at[slot], G_h.at[at + slot], sg.at[slot, 0]),
            pltpu.make_async_copy(Gd.at[slot], half, sg.at[slot, 1]),
        ]

    starts(wcp)(0)
    gacc[...] = jnp.zeros_like(gacc)
    for one in first:
        one.wait()

    def chunk(c, _):
        waits(wcp)(c)

        @pl.when(c < chunks - 1)
        def _next():
            starts(wcp)(c + 1)

        @pl.when(c >= 2)
        def _free():
            waits(gcp)(c - 2)

        slot = c % 2
        feed_chunk(n2, cot, W.at[slot], Wd.at[slot], G.at[slot], Gd.at[slot], hid, dgu, oacc, gacc)
        starts(gcp)(c)
        return 0

    lax.fori_loop(0, chunks, chunk, 0)
    n2[...] = oacc[...].astype(BF)
    c1 = pltpu.make_async_copy(n2, out_h, s.at[0])
    c1.start()
    feed_finish(gacc, mixed, cot, vec, vecs, oacc)
    c2 = pltpu.make_async_copy(oacc, gm_h, s.at[1])
    c3 = pltpu.make_async_copy(vecs, vecs_h, s.at[2])
    c2.start()
    c3.start()
    waits(gcp)(chunks - 2)
    waits(gcp)(chunks - 1)
    c1.wait()
    c2.wait()
    c3.wait()


def feed_finish(gacc, mixed, cot, vec, vecs, gm):
    vecs[...] = jnp.zeros_like(vecs)

    def block(r, _):
        rows = pl.ds(pl.multiple_of(r * BLK, BLK), BLK)
        hat, rstd = hat_of(mixed[rows, :])
        grad = gacc[rows, :]
        vecs[0:1, :] += jnp.sum(grad * hat, axis=0, keepdims=True)
        vecs[1:2, :] += jnp.sum(grad, axis=0, keepdims=True)
        gm[rows, :] = cot[rows, :].astype(F32) + norm_back(grad, hat, rstd, vec[2:3, :])
        return 0

    lax.fori_loop(0, mixed.shape[0] // BLK, block, 0)


def run_b(n2, cot, mixed, vec, W):
    T, D = n2.shape
    sds = jax.ShapeDtypeStruct
    half = D // 2
    return pl.pallas_call(
        kernel_b,
        name="feed_forward",
        out_shape=[sds((T, D), BF), sds((T, D), F32), sds((8, D), F32), sds(W.shape, BF)],
        in_specs=[ANY] * 5,
        out_specs=[ANY] * 4,
        scratch_shapes=[
            pltpu.VMEM((T, D), BF), pltpu.VMEM((T, D), BF), pltpu.VMEM((T, D), F32), pltpu.VMEM(vec.shape, F32),
            pltpu.VMEM((T, D), F32), pltpu.VMEM((T, D), F32), pltpu.VMEM((2, ZN, 256, D), BF), pltpu.VMEM((2, ZN, 128, D), BF),
            pltpu.VMEM((T, half), BF), pltpu.VMEM((T, D), BF), pltpu.VMEM((2, ZN, 256, D), BF), pltpu.VMEM((2, ZN, 128, D), BF),
            pltpu.VMEM((8, D), F32),
            pltpu.SemaphoreType.DMA((5,)), pltpu.SemaphoreType.DMA((2, 2)), pltpu.SemaphoreType.DMA((2, 2)),
        ],
        compiler_params=pltpu.CompilerParams(vmem_limit_bytes=62 * MIB),
    )(n2, cot, mixed, vec, W)


def attention_backward(j, pair, qaug, kaug, vaug, doaug, dq, dk, dv):
    T = qaug.shape[0]
    low, high = max(0, j - 1) * BLK, min(T, (j + 2) * BLK)
    keys = slice(j * BLK, (j + 1) * BLK)
    sums = []
    for one in range(2):
        cols = pl.ds(pl.multiple_of((2 * pair + one) * 128, 128), 128)
        prob = jnp.exp2(nt(kaug[keys, cols], qaug[low:high, cols]))
        grad = nt(vaug[keys, cols], doaug[low:high, cols])
        prob_low = prob.astype(BF)
        gs = (prob * grad).astype(BF)
        sums.append((
            nn(prob_low, doaug[low:high, cols]),
            nn(gs, qaug[low:high, cols]),
            tn(gs, kaug[keys, cols]),
        ))
    left = lanes((BLK, 128)) < HEAD
    dv[keys, :] = jnp.where(left, sums[0][0], sums[1][0])
    dk[keys, :] = jnp.where(left, sums[0][1], sums[1][1]) * (1.0 / LOG2E)
    left = lanes((high - low, 128)) < HEAD
    dq[low:high, :] += jnp.where(left, sums[0][2], sums[1][2]) * (1.0 / math.sqrt(HEAD))


def head_grads(gm, att, W, doaug):
    T, D = gm.shape

    def block(j, _):
        flat = nt(gm[...].astype(BF), W[j])
        lane = lanes((T, 128))
        left = lane < HEAD
        for p in range(2):
            grad = flat[:, 128 * p : 128 * p + 128].astype(BF).astype(F32)
            prod = grad * att[:, pl.ds(pl.multiple_of(j * 256 + 128 * p, 128), 128)].astype(F32)
            for one in range(2):
                own = left if one == 0 else lane >= HEAD
                dot = jnp.sum(jnp.where(own, prod, 0.0), axis=-1, keepdims=True)
                base = HEAD if one == 0 else 0
                kept = jnp.where(own, grad, 0.0)
                for k, part in enumerate(split_three(-dot)):
                    kept = jnp.where(lane == base + 8 + k, part, kept)
                at = (4 * j + 2 * p + one) * 128
                doaug[:, pl.ds(pl.multiple_of(at, 128), 128)] = kept.astype(BF)
        return 0

    lax.fori_loop(0, D // 256, block, 0)


def backward_pair(pair, qaug, kaug, vaug, doaug, dq, dk, dv, cos, sin, dqkv):
    T = qaug.shape[0]
    dq[...] = jnp.zeros_like(dq)
    for j in range(T // BLK):
        attention_backward(j, pair, qaug, kaug, vaug, doaug, dq, dk, dv)
    cols = pl.ds(pl.multiple_of(pair * 128, 128), 128)
    dqkv[0, :, cols] = unturn(dq[...], cos[...], sin[...]).astype(BF)
    dqkv[1, :, cols] = unturn(dk[...], cos[...], sin[...]).astype(BF)
    dqkv[2, :, cols] = dv[...].astype(BF)


def input_finish(gn1, x, gm, vec, vecs):
    vecs[...] = jnp.zeros_like(vecs)

    def rows_of(r, _):
        rows = pl.ds(pl.multiple_of(r * BLK, BLK), BLK)
        hat, rstd = hat_of(x[rows, :].astype(F32))
        grad = gn1[rows, :]
        vecs[0:1, :] += jnp.sum(grad * hat, axis=0, keepdims=True)
        vecs[1:2, :] += jnp.sum(grad, axis=0, keepdims=True)
        gm[rows, :] += norm_back(grad, hat, rstd, vec[0:1, :])
        return 0

    lax.fori_loop(0, x.shape[0] // BLK, rows_of, 0)


def kernel_c(
    tok_h, vec_h, cos_h, sin_h, W_h, gm_h, n1_h, att_h, qaug_h, kaug_h, vaug_h,
    ig_h, vecs_h, G_h,
    vec, cos, sin, W, gm, att, qaug, kaug, vaug, doaug, dq, dk, dv, n1, dqkv, gn1, G, vecs, sems, sw, sg,
):
    T, D = gm.shape
    first = copies(
        [
            (gm_h, gm), (att_h, att), (W_h.at[3], W.at[0]), (vec_h, vec), (cos_h, cos), (sin_h, sin),
            (qaug_h, qaug), (kaug_h, kaug), (vaug_h, vaug), (n1_h, n1),
        ],
        sems,
    )
    for one in first[:6]:
        one.wait()
    head_grads(gm, att, W.at[0], doaug)
    wcps = [pltpu.make_async_copy(W_h.at[k], W.at[k % 2], sw.at[k % 2]) for k in range(3)]
    wcps[0].start()
    wcps[1].start()
    G[0] = tn(att[...], gm[...].astype(BF)).astype(BF).reshape(ZN, D // ZN, D)
    gcps = [pltpu.make_async_copy(G.at[k % 2], G_h.at[(3, 0, 1, 2)[k]], sg.at[k % 2]) for k in range(4)]
    gcps[0].start()
    for one in first[6:]:
        one.wait()

    def per_pair(pair, _):
        backward_pair(pair, qaug, kaug, vaug, doaug, dq, dk, dv, cos, sin, dqkv)
        return 0

    lax.fori_loop(0, D // 128, per_pair, 0)
    tokc = pltpu.make_async_copy(tok_h, att, sems.at[0])
    tokc.start()
    for k in range(3):
        if k >= 1:
            gcps[k - 1].wait()
        G[(k + 1) % 2] = tn(n1[...], dqkv[k]).astype(BF).reshape(ZN, D // ZN, D)
        gcps[k + 1].start()
        wcps[k].wait()
        term = nt(dqkv[k], W[k % 2].reshape(D, D))
        gn1[...] = term if k == 0 else gn1[...] + term
        if k == 0:
            wcps[2].start()
    tokc.wait()
    input_finish(gn1, att, gm, vec, vecs)
    last = copies([(gm, ig_h), (vecs, vecs_h)], sems)
    gcps[2].wait()
    gcps[3].wait()
    for one in last:
        one.wait()


def run_c(tok, vec, cos, sin, W, gm, n1, att, qaug, kaug, vaug):
    T, D = tok.shape
    sds = jax.ShapeDtypeStruct
    v = pltpu.VMEM
    return pl.pallas_call(
        kernel_c,
        name="attention_backward",
        out_shape=[sds((T, D), F32), sds((8, D), F32), sds((4, ZN, D // ZN, D), BF)],
        in_specs=[ANY] * 11,
        out_specs=[ANY] * 3,
        scratch_shapes=[
            v(vec.shape, F32), v((T, 128), F32), v((T, 128), F32), v((2, ZN, D // ZN, D), BF), v((T, D), F32), v((T, D), BF),
            v((T, 2 * D), BF), v((T, 2 * D), BF), v((T, 2 * D), BF), v((T, 2 * D), BF),
            v((T, 128), F32), v((T, 128), F32), v((T, 128), F32), v((T, D), BF), v((3, T, D), BF), v((T, D), F32),
            v((2, ZN, D // ZN, D), BF), v((8, D), F32),
            pltpu.SemaphoreType.DMA((10,)), pltpu.SemaphoreType.DMA((2,)), pltpu.SemaphoreType.DMA((2,)),
        ],
        compiler_params=pltpu.CompilerParams(vmem_limit_bytes=62 * MIB),
    )(tok, vec, cos, sin, W, gm, n1, att, qaug, kaug, vaug)


def tables(lengths, row_len):
    order = jnp.arange(lengths.shape[-1], dtype=jnp.int32)
    ends = jnp.sum(jnp.where(order[:, None] <= order[None, :], lengths[0][:, None], 0), axis=0)
    starts = ends - lengths[0]
    places = jnp.arange(row_len, dtype=jnp.int32)[:, None]
    inside = (places >= starts[None, :]) & (places < ends[None, :])
    offset = jnp.sum(jnp.where(inside, starts[None, :], 0), axis=1, keepdims=True)
    lane = jnp.arange(128, dtype=jnp.int32)
    power = (lane % (HEAD // 2)).astype(F32) * (-2.0 / HEAD)
    inverse = jnp.power(jnp.float32(ROTARY_BASE), power)
    angles = (places - offset).astype(F32) * inverse[None, :]
    sign = jnp.where(lane % HEAD < HEAD // 2, -1.0, 1.0).astype(F32)
    place = lane % HEAD
    mine = jnp.sum(
        jnp.where(inside[:, None, :] & (order[None, None, :] == place[None, :, None]), 1.0, 0.0), axis=-1
    )
    aq = mine.astype(BF)
    ak = jnp.where(place < 8, (mine - 1.0) * 1e30, jnp.where(place < 11, 1.0, 0.0)).astype(BF)
    return jnp.cos(angles), jnp.sin(angles) * sign[None, :], aq, ak


def kernel_spread(fin_h, q_h, k_h, v_h, o_h, gate_h, up_h, down_h, fin, wide, sems, osems):
    n = fin_h.shape[0]
    load = [pltpu.make_async_copy(fin_h.at[p], fin.at[p], sems.at[p]) for p in range(n)]
    for copy in load:
        copy.start()
    out = []
    for p in range(n):
        load[p].wait()
        wide[p] = fin[p].astype(F32)
        made = []
        if p < 4:
            made.append((wide.at[p], (q_h, k_h, v_h, o_h)[p]))
        elif (p - 4) % 3 == 2:
            made.append((wide.at[p], down_h.at[pl.ds(256 * ((p - 4) // 3), 256)]))
        else:
            i = 2 * ((p - 4) // 3) + (p - 4) % 3
            for j in range(ZN):
                cols = pl.ds(1024 * j + 128 * i, 128)
                made.append((wide.at[p, :, pl.ds(128 * j, 128)], gate_h.at[:, cols]))
                made.append((wide.at[p, :, pl.ds(512 + 128 * j, 128)], up_h.at[:, cols]))
        out += [pltpu.make_async_copy(x, y, osems.at[p, i]) for i, (x, y) in enumerate(made)]
        for copy in out[-len(made) :]:
            copy.start()
    for copy in out:
        copy.wait()


def run_spread(fin, shapes):
    return pl.pallas_call(
        kernel_spread,
        name="spread_sums",
        out_shape=[jax.ShapeDtypeStruct(shape, F32) for shape in shapes],
        in_specs=[ANY],
        out_specs=[ANY] * len(shapes),
        scratch_shapes=[
            pltpu.VMEM(fin.shape, BF), pltpu.VMEM(fin.shape, F32),
            pltpu.SemaphoreType.DMA((16,)), pltpu.SemaphoreType.DMA((16, 8)),
        ],
        compiler_params=pltpu.CompilerParams(vmem_limit_bytes=40 * MIB),
    )(fin)


def sum_rest(part_sum):
    size, step = lax.axis_size("wide"), 8
    while step < size:
        pairs = [(i, (i // (2 * step)) * 2 * step + (i + step) % (2 * step)) for i in range(size)]
        other = lax.ppermute(part_sum, "wide", pairs)
        part_sum = (part_sum.astype(F32) + other.astype(F32)).astype(part_sum.dtype)
        step *= 2
    return part_sum


def shards(
    tokens, lengths, ln1_gain, ln1_bias, w_query, w_key, w_value, w_out,
    ln2_gain, ln2_bias, w_gate, w_up, w_down, cotangent,
):
    _rows, T, D = tokens.shape
    DR = D // ZN
    vectors = lax.all_gather(jnp.stack([ln1_gain, ln1_bias, ln2_gain, ln2_bias]), "narrow", axis=1, tiled=True)
    vec = jnp.concatenate([vectors.astype(F32), jnp.zeros((4, D), F32)])
    cos, sin, aq, ak = tables(lengths, T)
    W = run_gather(w_query, w_key, w_value, w_out, w_gate, w_up, w_down)
    tok, cot = tokens[0], cotangent[0]
    mixed, n2, n1, att, qaug, kaug, vaug = run_a(tok, vec, cos, sin, aq, ak, W)
    out, gm, vecs2, G_ffn = run_b(n2, cot, mixed, vec, W)
    input_grad, vecs1, G_attn = run_c(tok, vec, cos, sin, W, gm, n1, att, qaug, kaug, vaug)
    fin = sum_rest(run_reduce(G_attn, G_ffn))
    sums = run_spread(fin, [w.shape for w in (w_query, w_key, w_value, w_out, w_gate, w_up, w_down)])
    vector_sums = lax.psum(jnp.concatenate([vecs1[:2], vecs2[:2]]), ("wide", "narrow"))
    mine = lax.dynamic_slice_in_dim(vector_sums, lax.axis_index("narrow") * DR, DR, axis=1)
    return (out[None], input_grad[None], mine[0], mine[1], *sums[:4], mine[2], mine[3], *sums[4:])


def solution(mesh):
    both = ("wide", "narrow")
    row3, row2, vector, matrix = P(both, None, None), P(both, None), P("narrow"), P("narrow", None)
    weights = (vector, vector, matrix, matrix, matrix, matrix, vector, vector, matrix, matrix, matrix)
    return jax.shard_map(
        shards,
        mesh=mesh,
        in_specs=(row3, row2) + weights + (row3,),
        out_specs=(row3, row3) + weights,
        check_vma=False,
    )
```

```python
import functools
import math

import jax
import jax.numpy as jnp
import numpy as np
from jax import lax
from jax.experimental import pallas as pl
from jax.experimental.pallas import tpu as pltpu
from jax.sharding import PartitionSpec as P

F32 = jnp.float32
BF = jnp.bfloat16
HEAD = 64
BLK = 256
LOG2E = 1.4426950408889634
EPS = 1e-5
ROTARY_BASE = 10000.0
ANY = pl.BlockSpec(memory_space=pl.ANY)
MIB = 1024 * 1024
ZN = 4


def nn(a, b):
    return lax.dot_general(a, b, (((1,), (0,)), ((), ())), preferred_element_type=F32)


def nt(a, b):
    return lax.dot_general(a, b, (((1,), (1,)), ((), ())), preferred_element_type=F32)


def tn(a, b):
    return lax.dot_general(a, b, (((0,), (0,)), ((), ())), preferred_element_type=F32)


def lanes(shape):
    return lax.broadcasted_iota(jnp.int32, shape, len(shape) - 1)


def hat_of(x):
    center = x - jnp.mean(x, axis=-1, keepdims=True)
    rstd = lax.rsqrt(jnp.mean(center * center, axis=-1, keepdims=True) + EPS)
    return center * rstd, rstd


def norm_back(grad, hat, rstd, gain):
    scaled = grad * gain
    first = jnp.mean(scaled, axis=-1, keepdims=True)
    second = jnp.mean(scaled * hat, axis=-1, keepdims=True)
    return rstd * (scaled - first - hat * second)


def halves(u):
    first = lax.rem(lanes(u.shape), HEAD) < HEAD // 2
    ahead = pltpu.roll(u, u.shape[-1] - HEAD // 2, axis=u.ndim - 1)
    behind = pltpu.roll(u, HEAD // 2, axis=u.ndim - 1)
    return jnp.where(first, ahead, behind)


def turn(u, cos, sin_signed):
    return u * cos + halves(u) * sin_signed


def unturn(g, cos, sin_signed):
    return g * cos - halves(g) * sin_signed


def copies(pairs, sems):
    made = [pltpu.make_async_copy(a, b, sems.at[i]) for i, (a, b) in enumerate(pairs)]
    for one in made:
        one.start()
    return made


def split_three(v):
    top = v.astype(BF).astype(F32)
    rest = v - top
    mid = rest.astype(BF).astype(F32)
    return top, mid, rest - mid


MESH_ID = pl.DeviceIdType.MESH


def place():
    w, z = lax.axis_index("wide"), lax.axis_index("narrow")
    c, a, b = lax.rem(w, 2), lax.rem(w // 2, 2), lax.rem(w // 4, 2)
    lo, hi = lax.rem(z, 2), z // 2
    return dict(
        w=w, z=z, c=c, a=a, b=b, lo=lo, hi=hi,
        wc=w + 1 - 2 * c, wx=w + 2 - 4 * a, wy=w + 4 - 8 * b, zl=z + 1 - 2 * lo, zh=z + 2 - 4 * hi,
    )


def around(me, k):
    return lax.rem(me["z"] + k + ZN, ZN)


def remote(src, dst, ssem, rsem, w, z):
    return pltpu.make_async_remote_copy(
        src_ref=src, dst_ref=dst, send_sem=ssem, recv_sem=rsem, device_id=(w, z), device_id_type=MESH_ID
    )


def meet(me):
    barrier = pltpu.get_barrier_semaphore()
    others = [(me["wc"], me["z"]), (me["wx"], me["z"]), (me["wy"], me["z"])]
    others += [(me["w"], around(me, k)) for k in range(1, ZN)]
    for other in others:
        pl.semaphore_signal(barrier, inc=1, device_id=other, device_id_type=MESH_ID)
    pl.semaphore_wait(barrier, len(others))


def part(start, size):
    return pl.ds(pl.multiple_of(start, size), size)


LEFT, RIGHT = pl.ds(0, 512), pl.ds(512, 512)


class Gather:
    def __init__(self, me, first, dst, ssem, rsem):
        self.me, self.first, self.dst, self.ssem, self.rsem = me, first, dst, ssem, rsem
        c, a, b = me["c"], me["a"], me["b"]
        self.mine = part(c * 128 + a * 64 + b * 32, 32)
        self.from_x = part(c * 128 + (1 - a) * 64 + b * 32, 32)
        self.from_y = part(c * 128 + a * 64 + (1 - b) * 32, 32)
        self.core_half = part(c * 128, 128)

    def along(self, p, k, rows, cols, at, w, z, owner):
        ref = self.dst.at[p, owner, rows, cols]
        return remote(ref, ref, self.ssem.at[p, at + k - 1], self.rsem.at[p, at + k - 1], w, z)

    def z_copy(self, p, k):
        me = self.me
        own = self.first[p] if isinstance(p, int) and p < len(self.first) else self.dst.at[p, me["z"]]
        src, dst = own.at[self.mine], self.dst.at[p, me["z"], self.mine]
        return remote(src, dst, self.ssem.at[p, k - 1], self.rsem.at[p, k - 1], me["w"], around(me, k))

    def x_copy(self, p, k):
        return self.along(p, k, self.mine, pl.ds(0, 1024), 3, self.me["wx"], self.me["z"], around(self.me, -k))

    def y_copy(self, p, k):
        return self.along(p, k, self.mine, pl.ds(0, 1024), 6, self.me["wy"], self.me["z"], around(self.me, -k))

    def xy_copy(self, p, k):
        return self.along(p, k, self.from_y, LEFT, 9, self.me["wx"], self.me["z"], around(self.me, -k))

    def yx_copy(self, p, k):
        return self.along(p, k, self.from_x, RIGHT, 12, self.me["wy"], self.me["z"], around(self.me, -k))

    def core_copy(self, p, k):
        return self.along(p, k, self.core_half, pl.ds(0, 1024), 15, self.me["wc"], self.me["z"], around(self.me, -k))

    def start_z(self, p):
        for k in range(1, ZN):
            self.z_copy(p, k).start()

    def stage_one(self, p):
        for k in range(1, ZN):
            self.z_copy(p, k).wait_recv()
            self.x_copy(p, k).start()
            self.y_copy(p, k).start()

    def stage_two(self, p):
        for k in range(1, ZN):
            self.y_copy(p, k).wait_recv()
            self.xy_copy(p, k).start()
            self.x_copy(p, k).wait_recv()
            self.yx_copy(p, k).start()

    def stage_core(self, p):
        for k in range(1, ZN):
            self.xy_copy(p, k).wait_recv()
            self.yx_copy(p, k).wait_recv()
            self.core_copy(p, k).start()

    def finish(self, p):
        for k in range(1, ZN):
            self.core_copy(p, k).wait_recv()
        for k in range(1, ZN):
            for copy in (self.z_copy, self.x_copy, self.y_copy, self.xy_copy, self.yx_copy, self.core_copy):
                copy(p, k).wait_send()


    def slot(self, t):
        n = self.dst.shape[0]
        for stage, lag in ((self.finish, 4), (self.stage_core, 3), (self.stage_two, 2), (self.stage_one, 1)):
            p = t - lag

            def due(stage=stage, p=p):
                stage(p)

            when((p >= 0) & (p < n), due)

        def begin():
            self.start_z(t)

        when((t >= len(self.first)) & (t < n), begin)


def add_up(*parts):
    total = parts[0].astype(F32)
    for one in parts[1:]:
        total = total + one.astype(F32)
    return total.astype(BF)


def when(cond, body):
    if isinstance(cond, bool):
        if cond:
            body()
    else:
        pl.when(cond)(body)


class Reduce:
    SCRATCH = [
        ((2, 4, 128, 1024), "g0"), ((2, 4, 128, 1024), "r0"), ((4, 128, 1024), "s0"), ((2, 2, 4, 64, 512), "r1"),
        ((2, 2, 2, 64, 512), "s1"), ((2, 2, 2, 64, 512), "r2"), ((2, 2, 64, 512), "s2"), ((2, 2, 64, 512), "r3"),
        ((2, 64, 512), "s3"), ((2, 2, 32, 512), "r4"), ((2, 2, 32, 512), "f"),
    ]
    LAST = 7

    def __init__(self, me, G, fin, bufs, ssem, rsem, lsem):
        self.me, self.G, self.fin, self.ssem, self.rsem, self.lsem = me, G, fin, ssem, rsem, lsem
        for (_shape, name), ref in zip(self.SCRATCH, bufs):
            setattr(self, name, ref)

    def to(self, p, i, src, dst, w, z=None):
        z = self.me["z"] if z is None else z
        slot = lax.rem(p, 2)
        return remote(src, dst, self.ssem.at[slot, i], self.rsem.at[slot, i], w, z)

    def copies(self, s, p):
        me = self.me
        a, b, c, slot = me["a"], me["b"], me["c"], lax.rem(p, 2)
        every = pl.ds(0, ZN)
        if s == 0:
            return [
                self.to(p, 0, self.G.at[p, every, part((1 - c) * 128, 128)], self.r0.at[slot], me["wc"]),
                pltpu.make_async_copy(self.G.at[p, every, part(c * 128, 128)], self.g0.at[slot], self.lsem.at[slot, 2]),
            ]
        if s == 1:
            return [
                self.to(p, 1, self.s0.at[every, part((1 - a) * 64, 64), LEFT], self.r1.at[slot, 0], me["wx"]),
                self.to(p, 2, self.s0.at[every, part((1 - b) * 64, 64), RIGHT], self.r1.at[slot, 1], me["wy"]),
            ]
        if s == 2:
            return [self.to(p, 3, self.s1.at[1 - me["lo"]], self.r2.at[slot], me["w"], me["zl"])]
        if s == 3:
            return [self.to(p, 4, self.s2.at[1 - me["hi"]], self.r3.at[slot], me["w"], me["zh"])]
        if s == 4:
            return [
                self.to(p, 5, self.s3.at[0, part((1 - b) * 32, 32)], self.r4.at[slot, 0], me["wy"]),
                self.to(p, 6, self.s3.at[1, part((1 - a) * 32, 32)], self.r4.at[slot, 1], me["wx"]),
            ]
        if s == 5:
            left = self.fin.at[p, part(c * 128 + a * 64 + b * 32, 32), LEFT]
            right = self.fin.at[p, part(c * 128 + b * 64 + a * 32, 32), RIGHT]
            return [
                self.to(p, 7, self.f.at[slot, 0], left, me["wy"]),
                self.to(p, 8, self.f.at[slot, 1], right, me["wx"]),
                pltpu.make_async_copy(self.f.at[slot, 0], left, self.lsem.at[slot, 0]),
                pltpu.make_async_copy(self.f.at[slot, 1], right, self.lsem.at[slot, 1]),
            ]
        if s == 6:
            left = self.fin.at[p, part(c * 128 + a * 64, 64), LEFT]
            right = self.fin.at[p, part(c * 128 + b * 64, 64), RIGHT]
            return [self.to(p, 9, left, left, me["wx"]), self.to(p, 10, right, right, me["wy"])]
        half = self.fin.at[p, part(c * 128, 128)]
        return [self.to(p, 11, half, half, me["wc"])]

    def start(self, s, p):
        for copy in self.copies(s, p):
            copy.start()

    def advance(self, s, p):
        for copy in self.copies(s, p):
            copy.wait()
        me = self.me
        a, b, slot = me["a"], me["b"], lax.rem(p, 2)
        if s == 0:
            for k in range(ZN):
                self.s0[k] = add_up(self.g0[slot, k], self.r0[slot, k])
        if s == 1:
            for k in range(ZN):
                self.s1[k % 2, 0, k // 2] = add_up(self.s0[k, part(a * 64, 64), 0:512], self.r1[slot, 0, k])
                self.s1[k % 2, 1, k // 2] = add_up(self.s0[k, part(b * 64, 64), 512:1024], self.r1[slot, 1, k])
        if s == 2:
            for hi in range(2):
                for side in range(2):
                    self.s2[hi, side] = add_up(self.s1[me["lo"], side, hi], self.r2[slot, side, hi])
        if s == 3:
            self.s3[...] = add_up(self.s2[me["hi"]], self.r3[slot])
        if s == 4:
            self.f[slot, 0] = add_up(self.s3[0, part(b * 32, 32), :], self.r4[slot, 0])
            self.f[slot, 1] = add_up(self.s3[1, part(a * 32, 32), :], self.r4[slot, 1])
        if s < self.LAST:
            self.start(s + 1, p)

    def slot(self, t, n):
        for s in range(self.LAST, -1, -1):
            p = t - 1 - s

            def due(s=s, p=p):
                self.advance(s, p)

            when((p >= 0) & (p < n), due)

        def begin():
            self.start(0, t)

        when(t < n, begin)


def loop(n, body):
    def step(i, _):
        body(i)
        return 0

    lax.fori_loop(0, n, step, 0)


def starts(make):
    def body(i):
        made = make(i)
        for copy in made if isinstance(made, list) else [made]:
            copy.start()

    return body


def waits(make):
    def body(i):
        made = make(i)
        for copy in made if isinstance(made, list) else [made]:
            copy.wait()

    return body


def attention_forward(i, pair, qaug, kaug, vaug, att):
    T = qaug.shape[0]
    low, high = max(0, i - 1) * BLK, min(T, (i + 2) * BLK)
    rows = slice(i * BLK, (i + 1) * BLK)
    outs, tops = [], []
    for one in range(2):
        cols = pl.ds(pl.multiple_of((2 * pair + one) * 128, 128), 128)
        scores = nt(qaug[rows, cols], kaug[low:high, cols])
        top = jnp.max(scores, axis=-1, keepdims=True)
        raised = jnp.exp2(scores - top).astype(BF)
        outs.append(nn(raised, vaug[low:high, cols]))
        tops.append(top)
    lane = lanes((BLK, 128))
    left = lane < HEAD
    for one in range(2):
        cols = pl.ds(pl.multiple_of((2 * pair + one) * 128, 128), 128)
        base = HEAD if one == 0 else 0
        parts = split_three(-(tops[one] + jnp.log2(outs[one])))
        kept = qaug[rows, cols].astype(F32)
        for k, term in enumerate(parts):
            kept = jnp.where(lane == base + 8 + k, term, kept)
        qaug[rows, cols] = kept.astype(BF)
    summed = pltpu.roll(jnp.where(left, outs[1], outs[0]), HEAD, axis=1)
    att[rows, pl.ds(pl.multiple_of(pair * 128, 128), 128)] = (
        jnp.where(left, outs[0], outs[1]) / summed
    ).astype(BF)


def project_turned(n1, W, cos, sin, aug, dest, scale):
    T = n1.shape[0]

    def block(j, _):
        flat = nn(n1[...], W[:, :, part(j * 256, 256)].reshape(n1.shape[1], 256))
        left = lanes((T, 128)) < HEAD
        for p in range(2):
            u = turn(flat[:, 128 * p : 128 * p + 128], cos[...], sin[...])
            if scale != 1.0:
                u = u * scale
            extra = aug[...].astype(F32)
            at = (4 * j + 2 * p) * 128
            dest[:, pl.ds(pl.multiple_of(at, 128), 128)] = jnp.where(left, u, extra).astype(BF)
            dest[:, pl.ds(pl.multiple_of(at + 128, 128), 128)] = jnp.where(left, extra, u).astype(BF)
        return 0

    lax.fori_loop(0, n1.shape[1] // 256, block, 0)


def project_values(n1, W, dest):
    T = n1.shape[0]

    def block(j, _):
        flat = nn(n1[...], W[:, :, part(j * 256, 256)].reshape(n1.shape[1], 256))
        left = lanes((T, 128)) < HEAD
        for p in range(2):
            u = flat[:, 128 * p : 128 * p + 128]
            at = (4 * j + 2 * p) * 128
            dest[:, pl.ds(pl.multiple_of(at, 128), 128)] = jnp.where(left, u, 1.0).astype(BF)
            dest[:, pl.ds(pl.multiple_of(at + 128, 128), 128)] = jnp.where(left, 1.0, u).astype(BF)
        return 0

    lax.fori_loop(0, n1.shape[1] // 256, block, 0)


def norm_rows(source, dest, gain, bias, n=BLK):
    def block(r, _):
        rows = pl.ds(pl.multiple_of(r * n, n), n)
        hat, _unused = hat_of(source[rows, :].astype(F32))
        dest[rows, :] = (hat * gain + bias).astype(BF)
        return 0

    lax.fori_loop(0, source.shape[0] // n, block, 0)


def feed_values(n2, cot, gate_up, down, hid, dgu):
    D = n2.shape[1]
    half = hid.shape[1]
    gu = nn(n2[...], gate_up[...].reshape(D, 2 * half))
    g = gu[:, :half]
    u = gu[:, half:]
    gh = nt(cot[...], down[...].reshape(half, D))
    sig = 0.5 * jnp.tanh(0.5 * g) + 0.5
    silu = g * sig
    hid[...] = (silu * u).astype(BF)
    dgu[:, :half] = (gh * u * (sig + silu * (1.0 - sig))).astype(BF)
    dgu[:, half:] = (gh * silu).astype(BF)


def feed_sums(gate_up, down, hid, dgu, oacc, gacc):
    half, D = hid.shape[1], dgu.shape[1]
    oacc[...] += nn(hid[...], down[...].reshape(half, D))
    gacc[...] += nt(dgu[...], gate_up[...].reshape(D, 2 * half))


def feed_finish(gacc, mixed, cot, vec, vecs):
    def block(r, _):
        rows = pl.ds(pl.multiple_of(r * BLK, BLK), BLK)
        hat, rstd = hat_of(mixed[rows, :])
        grad = gacc[rows, :]
        vecs[2:3, :] += jnp.sum(grad * hat, axis=0, keepdims=True)
        vecs[3:4, :] += jnp.sum(grad, axis=0, keepdims=True)
        mixed[rows, :] = cot[rows, :].astype(F32) + norm_back(grad, hat, rstd, vec[2:3, :])
        return 0

    lax.fori_loop(0, mixed.shape[0] // BLK, block, 0)


def attention_backward(j, pair, qaug, kaug, vaug, doaug, dq, dk, dv):
    T = qaug.shape[0]
    low, high = max(0, j - 1) * BLK, min(T, (j + 2) * BLK)
    keys = slice(j * BLK, (j + 1) * BLK)
    sums = []
    for one in range(2):
        cols = pl.ds(pl.multiple_of((2 * pair + one) * 128, 128), 128)
        prob = jnp.exp2(nt(kaug[keys, cols], qaug[low:high, cols]))
        grad = nt(vaug[keys, cols], doaug[low:high, cols])
        prob_low = prob.astype(BF)
        gs = (prob * grad).astype(BF)
        sums.append((
            nn(prob_low, doaug[low:high, cols]),
            nn(gs, qaug[low:high, cols]),
            tn(gs, kaug[keys, cols]),
        ))
    left = lanes((BLK, 128)) < HEAD
    dv[keys, :] = jnp.where(left, sums[0][0], sums[1][0])
    dk[keys, :] = jnp.where(left, sums[0][1], sums[1][1]) * (1.0 / LOG2E)
    left = lanes((high - low, 128)) < HEAD
    dq[low:high, :] += jnp.where(left, sums[0][2], sums[1][2]) * (1.0 / math.sqrt(HEAD))


def head_grads(grad_res, att, W, doaug):
    T, D = grad_res.shape

    def block(j, _):
        flat = nt(grad_res[...], W[j])
        lane = lanes((T, 128))
        left = lane < HEAD
        for p in range(2):
            grad = flat[:, 128 * p : 128 * p + 128].astype(BF).astype(F32)
            prod = grad * att[:, :, part(j * 256 + 128 * p, 128)].reshape(T, 128).astype(F32)
            for one in range(2):
                own = left if one == 0 else lane >= HEAD
                dot = jnp.sum(jnp.where(own, prod, 0.0), axis=-1, keepdims=True)
                base = HEAD if one == 0 else 0
                kept = jnp.where(own, grad, 0.0)
                for k, term in enumerate(split_three(-dot)):
                    kept = jnp.where(lane == base + 8 + k, term, kept)
                at = (4 * j + 2 * p + one) * 128
                doaug[:, pl.ds(pl.multiple_of(at, 128), 128)] = kept.astype(BF)
        return 0

    lax.fori_loop(0, D // 256, block, 0)


def backward_pair(pair, qaug, kaug, vaug, doaug, dq, dk, dv, cos, sin, dqkv):
    T = qaug.shape[0]
    dq[...] = jnp.zeros_like(dq)
    for j in range(T // BLK):
        attention_backward(j, pair, qaug, kaug, vaug, doaug, dq, dk, dv)
    cols = pl.ds(pl.multiple_of(pair * 128, 128), 128)
    dqkv[0][:, cols] = unturn(dq[...], cos[...], sin[...]).astype(BF)
    dqkv[1][:, cols] = unturn(dk[...], cos[...], sin[...]).astype(BF)
    dqkv[2][:, cols] = dv[...].astype(BF)


def input_finish(gn1, x, gm, vec, vecs):
    def rows_of(r, _):
        rows = pl.ds(pl.multiple_of(r * BLK, BLK), BLK)
        hat, rstd = hat_of(x[rows, :].astype(F32))
        grad = gn1[rows, :]
        vecs[0:1, :] += jnp.sum(grad * hat, axis=0, keepdims=True)
        vecs[1:2, :] += jnp.sum(grad, axis=0, keepdims=True)
        gm[rows, :] += norm_back(grad, hat, rstd, vec[0:1, :])
        return 0

    lax.fori_loop(0, x.shape[0] // BLK, rows_of, 0)


CHUNKS = 8


def kernel_layer(
    tok_h, cot_h, vec_h, cos_h, sin_h, aq_h, ak_h, wq_h, wk_h, wv_h, wo_h, gate_h, up_h, down_h,
    out_h, ig_h, vsum_h, fin_h, dst, G_h, n1_h, att_h, mixed_h,
    F0, F1, Q, K, V, DO, PB, b0, b1, b2, GO, GD, dq, dk, dv, cos, sin, aq, ak, vec, vecs, vgot, *rest,
):
    bufs, (lsem, fsem, wsem, gsem, gssem, grsem, rssem, rrsem, rlsem, vssem, vrsem) = rest[:11], rest[11:]
    T, D = b0.shape
    me = place()
    z = me["z"]
    used = [0]

    def cp(src, dst_ref):
        copy = pltpu.make_async_copy(src, dst_ref, lsem.at[used[0]])
        used[0] += 1
        copy.start()
        return copy

    own_weights = (wq_h, wk_h, wv_h, wo_h)
    c_vec = cp(vec_h, vec.at[:, part(z * 256, 256)])
    c_tok = cp(tok_h, b0)
    c_own = [cp(own_weights[i], PB.at[i, z]) for i in range(4)]
    c_tables = [cp(cos_h, cos), cp(sin_h, sin), cp(aq_h, aq), cp(ak_h, ak)]
    c_down = cp(down_h, b1)

    def feed_in(i):
        made = []
        rows = part(256 * lax.rem(i, 4), 256)
        for j in range(ZN):
            cols = part(1024 * j + 128 * i, 128)
            for k, source in enumerate((gate_h, up_h)):
                to = part(1024 * (i // 4) + 512 * k + 128 * j, 128)
                made.append(pltpu.make_async_copy(source.at[:, cols], DO.at[rows, to], fsem.at[i, 2 * j + k]))
        return made

    def feed_out(i):
        at = 4 + 3 * (i // 2) + lax.rem(i, 2)
        source = DO.at[part(256 * lax.rem(i, 4), 256), part(1024 * (i // 4), 1024)]
        return pltpu.make_async_copy(source, dst.at[at, z], fsem.at[i, 0])

    def down_out(i):
        return pltpu.make_async_copy(b1.at[part(256 * i, 256)], dst.at[6 + 3 * i, z], fsem.at[i, 1])

    loop(CHUNKS, starts(feed_in))
    meet(me)
    g = Gather(me, own_weights, dst, gssem, grsem)
    r = Reduce(me, G_h, fin_h, bufs, rssem, rrsem, rlsem)

    def vec_copy(k):
        return remote(vec_h, vec.at[:, part(z * 256, 256)], vssem.at[k - 1], vrsem.at[k - 1], me["w"], around(me, k))

    for k in range(1, ZN):
        vec_copy(k).start()
    for p in range(4):
        g.start_z(p)
    loop(CHUNKS, waits(feed_in))
    loop(CHUNKS, starts(feed_out))
    c_down.wait()
    loop(4, starts(down_out))
    c_own_out = []
    for i in range(4):
        c_own[i].wait()
        c_own_out.append(cp(PB.at[i, z], dst.at[i, z]))
    c_tok.wait()
    c_vec.wait()
    for k in range(1, ZN):
        vec_copy(k).wait()
    norm_rows(b0, b2, vec[0:1, :], vec[1:2, :])
    c_n1 = [cp(b2.at[pl.ds(256 * k, 256)], n1_h.at[k]) for k in range(ZN)]
    for one in c_tables:
        one.wait()

    def bring(p):
        return [cp(dst.at[p, around(me, k)], PB.at[p, around(me, k)]) for k in range(1, ZN)]

    g.slot(1)
    g.slot(2)
    g.slot(3)
    loop(CHUNKS, waits(feed_out))
    loop(4, waits(down_out))
    g.slot(4)
    for one in bring(0):
        one.wait()
    project_turned(b2, PB.at[0], cos, sin, aq, Q, LOG2E / math.sqrt(HEAD))
    g.slot(5)
    for one in bring(1):
        one.wait()
    project_turned(b2, PB.at[1], cos, sin, ak, K, 1.0)
    g.slot(6)
    for one in bring(2):
        one.wait()
    project_values(b2, PB.at[2], V)
    g.slot(7)
    c_out_weight = bring(3)

    def pair_forward(pair, _):
        for i in range(T // BLK):
            attention_forward(i, pair, Q, K, V, b1)

        @pl.when(lax.rem(pair, 2) == 1)
        def _gather():
            g.slot(8 + pair // 2)

        return 0

    lax.fori_loop(0, D // 128, pair_forward, 0)
    c_att = [cp(b1.at[pl.ds(256 * k, 256)], att_h.at[k]) for k in range(ZN)]
    for one in c_out_weight + c_own_out + c_n1:
        one.wait()
    F0[...] = b0[...].astype(F32) + nn(b1[...], PB[3].reshape(D, D))

    def load(c):
        at, slot = 4 + 3 * (c // 2), lax.rem(c, 2)
        return pltpu.make_async_copy(dst.at[at + slot], PB.at[slot], wsem.at[slot])

    def load_down(c):
        slot = lax.rem(c // 2, 2)
        return pltpu.make_async_copy(dst.at[6 + 3 * (c // 2)], PB.at[2 + slot], wsem.at[2 + slot])

    load(jnp.int32(0)).start()
    load_down(jnp.int32(0)).start()
    c_mixed = cp(F0, mixed_h)
    c_cot = cp(cot_h, b0)
    g.slot(12)
    norm_rows(F0, b2, vec[2:3, :], vec[3:4, :])
    for one in c_att + [c_mixed, c_cot]:
        one.wait()
    F1[...] = jnp.zeros_like(F1)
    hid, dgu = DO.at[:, pl.ds(D, D // 2)], DO.at[:, pl.ds(0, D)]

    def stored(c):
        at, slot = 3 * (c // 2), lax.rem(c, 2)
        return [
            pltpu.make_async_copy(GO, G_h.at[at + slot], gsem.at[0]),
            pltpu.make_async_copy(GD, G_h.at[at + 2, :, part(slot * 128, 128)], gsem.at[1]),
        ]

    def chunk(c, _):
        slot = lax.rem(c, 2)
        load(c).wait()

        @pl.when(slot == 0)
        def _down():
            load_down(c).wait()

        @pl.when(c < CHUNKS - 1)
        def _next():
            load(c + 1).start()

        @pl.when((c < CHUNKS - 1) & (slot == 1))
        def _next_down():
            load_down(c + 1).start()

        gate_up = PB.at[slot]
        down = PB.at[2 + lax.rem(c // 2, 2), :, part(slot * 128, 128)]
        feed_values(b2, b0, gate_up, down, hid, dgu)
        g.slot(13 + 2 * c)
        feed_sums(gate_up, down, hid, dgu, F0, F1)

        @pl.when(c >= 1)
        def _sums():
            waits(stored)(c - 1)
            r.slot(c - 1, 16)

        GO[...] = tn(b2[...], dgu[...]).astype(BF).reshape(GO.shape)
        GD[...] = tn(hid[...], b0[...]).astype(BF).reshape(GD.shape)
        starts(stored)(c)
        g.slot(14 + 2 * c)
        return 0

    lax.fori_loop(0, CHUNKS, chunk, 0)

    def whole(source, slot):
        return cp(source, PB.at[slot])

    c_wo = whole(dst.at[3], 2)
    c_att = whole(att_h, 0)
    c_n1 = whole(n1_h, 1)
    b1[...] = F0[...].astype(BF)
    c_out = cp(b1, out_h)
    c_mixed = cp(mixed_h, F0)
    waits(stored)(CHUNKS - 1)
    r.slot(jnp.int32(7), 16)
    c_mixed.wait()
    vecs[...] = jnp.zeros_like(vecs)
    feed_finish(F1, F0, b0, vec, vecs)
    b2[...] = F0[...].astype(BF)

    c_wo.wait()
    c_att.wait()
    head_grads(b2, PB.at[0], PB.at[2], DO)
    GO[...] = tn(PB[0].reshape(T, D), b2[...]).astype(BF).reshape(GO.shape)
    c_go = cp(GO, G_h.at[12])
    c_wq = whole(dst.at[0], 3)
    c_wk = whole(dst.at[1], 0)
    c_wv = whole(dst.at[2], 2)
    r.slot(jnp.int32(8), 16)
    c_go.wait()
    c_out.wait()

    def pair_backward(pair, _):
        backward_pair(pair, Q, K, V, DO, dq, dk, dv, cos, sin, (b0, b1, b2))

        @pl.when(lax.rem(pair, 2) == 1)
        def _sums():
            r.slot(9 + pair // 2, 16)

        return 0

    lax.fori_loop(0, D // 128, pair_backward, 0)
    c_n1.wait()
    for k, (grad, weight, at) in enumerate(((b0, c_wq, 3), (b1, c_wk, 0), (b2, c_wv, 2))):
        GO[...] = tn(PB[1].reshape(T, D), grad[...]).astype(BF).reshape(GO.shape)
        c_go = cp(GO, G_h.at[13 + k])
        weight.wait()
        term = nt(grad[...], PB[at].reshape(D, D))
        F1[...] = term if k == 0 else F1[...] + term
        c_go.wait()
        r.slot(jnp.int32(13 + k), 16)
        if k == 0:
            c_tok = cp(tok_h, b0)
    c_tok.wait()
    r.slot(jnp.int32(16), 16)
    input_finish(F1, b0, F0, vec, vecs)
    c_ig = cp(F0, ig_h)

    steps = [(me["wc"], z), (me["wx"], z), (me["wy"], z), (me["w"], me["zl"]), (me["w"], me["zh"])]

    def vec_step(i):
        return remote(vecs, vgot.at[i], vssem.at[3 + i], vrsem.at[3 + i], steps[i][0], steps[i][1])

    vec_step(0).start()
    for t in range(17, 24):
        i = t - 17
        if i < 5:
            vec_step(i).wait()
            vecs[...] += vgot[i]
            if i < 4:
                vec_step(i + 1).start()
        r.slot(jnp.int32(t), 16)
    c_vs = cp(vecs, vsum_h)
    c_vs.wait()
    c_ig.wait()


def run_layer(tok, cot, vec, cos, sin, aq, ak, *weights):
    T, D = tok.shape
    sds, v, sem = jax.ShapeDtypeStruct, pltpu.VMEM, pltpu.SemaphoreType.DMA
    piece = (ZN, 256, D)
    return pl.pallas_call(
        kernel_layer,
        name="layer",
        out_shape=[
            sds((T, D), BF), sds((T, D), F32), sds((8, D), F32), sds((16, 256, D), BF), sds((16,) + piece, BF),
            sds((16,) + piece, BF), sds(piece, BF), sds(piece, BF), sds((T, D), F32),
        ],
        in_specs=[ANY] * 14,
        out_specs=[ANY] * 9,
        scratch_shapes=[
            v((T, D), F32), v((T, D), F32), v((T, 2 * D), BF), v((T, 2 * D), BF), v((T, 2 * D), BF), v((T, 2 * D), BF),
            v((4,) + piece, BF), v((T, D), BF), v((T, D), BF), v((T, D), BF), v(piece, BF), v((ZN, 128, D), BF),
            v((T, 128), F32), v((T, 128), F32), v((T, 128), F32), v((T, 128), F32), v((T, 128), F32),
            v((T, 128), BF), v((T, 128), BF), v((8, D), F32), v((8, D), F32), v((5, 8, D), F32),
        ]
        + [v(shape, BF) for shape, _ in Reduce.SCRATCH]
        + [
            sem((64,)), sem((8, 8)), sem((4,)), sem((2,)), sem((16, 18)), sem((16, 18)),
            sem((2, 12)), sem((2, 12)), sem((2, 3)), sem((8,)), sem((8,)),
        ],
        compiler_params=pltpu.CompilerParams(collective_id=0, has_side_effects=True, vmem_limit_bytes=63 * MIB),
    )(tok, cot, vec, cos, sin, aq, ak, *weights)


def tables(lengths, row_len):
    order = jnp.arange(lengths.shape[-1], dtype=jnp.int32)
    ends = jnp.sum(jnp.where(order[:, None] <= order[None, :], lengths[0][:, None], 0), axis=0)
    places = jnp.arange(row_len, dtype=jnp.int32)[:, None]
    before = places >= ends[None, :]
    segment = jnp.sum(before.astype(jnp.int32), axis=1, keepdims=True)
    offset = jnp.sum(jnp.where(before, lengths[0][None, :], 0), axis=1, keepdims=True)
    lane = jnp.arange(128, dtype=jnp.int32)
    power = (lane % (HEAD // 2)).astype(F32) * (-2.0 / HEAD)
    inverse = jnp.power(jnp.float32(ROTARY_BASE), power)
    angles = (places - offset).astype(F32) * inverse[None, :]
    sign = jnp.where(lane % HEAD < HEAD // 2, -1.0, 1.0).astype(F32)
    place = lane % HEAD
    mine = (segment == place[None, :]).astype(F32)
    aq = mine.astype(BF)
    ak = jnp.where(place < 8, (mine - 1.0) * 1e30, jnp.where(place < 11, 1.0, 0.0)).astype(BF)
    return jnp.cos(angles), jnp.sin(angles) * sign[None, :], aq, ak


def kernel_spread(fin_h, q_h, k_h, v_h, o_h, gate_h, up_h, down_h, fin, wide, sems, osems):
    n = fin_h.shape[0]
    load = [pltpu.make_async_copy(fin_h.at[p], fin.at[p], sems.at[p]) for p in range(n)]
    for copy in load:
        copy.start()
    out = []
    for p in range(n):
        load[p].wait()
        wide[p] = fin[p].astype(F32)
        made = []
        if p >= 12:
            made.append((wide.at[p], (o_h, q_h, k_h, v_h)[p - 12]))
        elif p % 3 == 2:
            made.append((wide.at[p], down_h.at[pl.ds(256 * (p // 3), 256)]))
        else:
            i = 2 * (p // 3) + p % 3
            for j in range(ZN):
                cols = pl.ds(1024 * j + 128 * i, 128)
                made.append((wide.at[p, :, pl.ds(128 * j, 128)], gate_h.at[:, cols]))
                made.append((wide.at[p, :, pl.ds(512 + 128 * j, 128)], up_h.at[:, cols]))
        out += [pltpu.make_async_copy(x, y, osems.at[p, i]) for i, (x, y) in enumerate(made)]
        for copy in out[-len(made) :]:
            copy.start()
    for copy in out:
        copy.wait()


def run_spread(fin, shapes):
    return pl.pallas_call(
        kernel_spread,
        name="spread_sums",
        out_shape=[jax.ShapeDtypeStruct(shape, F32) for shape in shapes],
        in_specs=[ANY],
        out_specs=[ANY] * len(shapes),
        scratch_shapes=[
            pltpu.VMEM(fin.shape, BF), pltpu.VMEM(fin.shape, F32),
            pltpu.SemaphoreType.DMA((16,)), pltpu.SemaphoreType.DMA((16, 8)),
        ],
        compiler_params=pltpu.CompilerParams(vmem_limit_bytes=40 * MIB),
    )(fin)


def sum_rest(part_sum):
    size, step = lax.axis_size("wide"), 8
    while step < size:
        pairs = [(i, (i // (2 * step)) * 2 * step + (i + step) % (2 * step)) for i in range(size)]
        other = lax.ppermute(part_sum, "wide", pairs)
        part_sum = (part_sum.astype(F32) + other.astype(F32)).astype(part_sum.dtype)
        step *= 2
    return part_sum


def shards(
    tokens, lengths, ln1_gain, ln1_bias, w_query, w_key, w_value, w_out,
    ln2_gain, ln2_bias, w_gate, w_up, w_down, cotangent,
):
    _rows, T, D = tokens.shape
    DR = D // ZN
    vec = jnp.stack([v.astype(F32) for v in (ln1_gain, ln1_bias, ln2_gain, ln2_bias)])
    vec = jnp.concatenate([vec, jnp.zeros_like(vec)])
    cos, sin, aq, ak = tables(lengths, T)
    weights = (w_query, w_key, w_value, w_out, w_gate, w_up, w_down)
    out, input_grad, vsum, fin = run_layer(tokens[0], cotangent[0], vec, cos, sin, aq, ak, *weights)[:4]
    sums = run_spread(sum_rest(fin), [w.shape for w in weights])
    mine = lax.dynamic_slice_in_dim(sum_rest(vsum), lax.axis_index("narrow") * DR, DR, axis=1)
    return (out[None], input_grad[None], mine[0], mine[1], *sums[:4], mine[2], mine[3], *sums[4:])


def solution(mesh):
    both = ("wide", "narrow")
    row3, row2, vector, matrix = P(both, None, None), P(both, None), P("narrow"), P("narrow", None)
    weights = (vector, vector, matrix, matrix, matrix, matrix, vector, vector, matrix, matrix, matrix)
    return jax.shard_map(
        shards,
        mesh=mesh,
        in_specs=(row3, row2) + weights + (row3,),
        out_specs=(row3, row3) + weights,
        check_vma=False,
    )
```

```python
import functools
import math

import jax
import jax.numpy as jnp
import numpy as np
from jax import lax
from jax.experimental import pallas as pl
from jax.experimental.pallas import tpu as pltpu
from jax.sharding import PartitionSpec as P

F32 = jnp.float32
BF = jnp.bfloat16
HEAD = 64
BLK = 256
LOG2E = 1.4426950408889634
EPS = 1e-5
ROTARY_BASE = 10000.0
ANY = pl.BlockSpec(memory_space=pl.ANY)
MIB = 1024 * 1024
ZN = 4


def nn(a, b):
    return lax.dot_general(a, b, (((1,), (0,)), ((), ())), preferred_element_type=F32)


def nt(a, b):
    return lax.dot_general(a, b, (((1,), (1,)), ((), ())), preferred_element_type=F32)


def tn(a, b):
    return lax.dot_general(a, b, (((0,), (0,)), ((), ())), preferred_element_type=F32)


def lanes(shape):
    return lax.broadcasted_iota(jnp.int32, shape, len(shape) - 1)


def hat_of(x):
    center = x - jnp.mean(x, axis=-1, keepdims=True)
    rstd = lax.rsqrt(jnp.mean(center * center, axis=-1, keepdims=True) + EPS)
    return center * rstd, rstd


def norm_back(grad, hat, rstd, gain):
    scaled = grad * gain
    first = jnp.mean(scaled, axis=-1, keepdims=True)
    second = jnp.mean(scaled * hat, axis=-1, keepdims=True)
    return rstd * (scaled - first - hat * second)


def halves(u):
    first = lax.rem(lanes(u.shape), HEAD) < HEAD // 2
    ahead = pltpu.roll(u, u.shape[-1] - HEAD // 2, axis=u.ndim - 1)
    behind = pltpu.roll(u, HEAD // 2, axis=u.ndim - 1)
    return jnp.where(first, ahead, behind)


def turn(u, cos, sin_signed):
    return u * cos + halves(u) * sin_signed


def unturn(g, cos, sin_signed):
    return g * cos - halves(g) * sin_signed


def copies(pairs, sems):
    made = [pltpu.make_async_copy(a, b, sems.at[i]) for i, (a, b) in enumerate(pairs)]
    for one in made:
        one.start()
    return made


def split_three(v):
    top = v.astype(BF).astype(F32)
    rest = v - top
    mid = rest.astype(BF).astype(F32)
    return top, mid, rest - mid


MESH_ID = pl.DeviceIdType.MESH


def place():
    w, z = lax.axis_index("wide"), lax.axis_index("narrow")
    c, a, b = lax.rem(w, 2), lax.rem(w // 2, 2), lax.rem(w // 4, 2)
    lo, hi = lax.rem(z, 2), z // 2
    return dict(
        w=w, z=z, c=c, a=a, b=b, lo=lo, hi=hi,
        wc=w + 1 - 2 * c, wx=w + 2 - 4 * a, wy=w + 4 - 8 * b, zl=z + 1 - 2 * lo, zh=z + 2 - 4 * hi,
    )


def around(me, k):
    return lax.rem(me["z"] + k + ZN, ZN)


def remote(src, dst, ssem, rsem, w, z):
    return pltpu.make_async_remote_copy(
        src_ref=src, dst_ref=dst, send_sem=ssem, recv_sem=rsem, device_id=(w, z), device_id_type=MESH_ID
    )


def meet(me):
    barrier = pltpu.get_barrier_semaphore()
    others = [(me["wc"], me["z"]), (me["wx"], me["z"]), (me["wy"], me["z"])]
    others += [(me["w"], around(me, k)) for k in range(1, ZN)]
    for other in others:
        pl.semaphore_signal(barrier, inc=1, device_id=other, device_id_type=MESH_ID)
    pl.semaphore_wait(barrier, len(others))


def part(start, size):
    return pl.ds(pl.multiple_of(start, size), size)


LEFT, RIGHT = pl.ds(0, 512), pl.ds(512, 512)


class Gather:
    def __init__(self, me, first, dst, ssem, rsem):
        self.me, self.first, self.dst, self.ssem, self.rsem = me, first, dst, ssem, rsem
        c, a, b = me["c"], me["a"], me["b"]
        self.mine = part(c * 128 + a * 64 + b * 32, 32)
        self.from_x = part(c * 128 + (1 - a) * 64 + b * 32, 32)
        self.from_y = part(c * 128 + a * 64 + (1 - b) * 32, 32)
        self.core_half = part(c * 128, 128)

    def along(self, p, k, rows, cols, at, w, z, owner):
        ref = self.dst.at[p, owner, rows, cols]
        return remote(ref, ref, self.ssem.at[p, at + k - 1], self.rsem.at[p, at + k - 1], w, z)

    def z_copy(self, p, k):
        me = self.me
        own = self.first[p] if isinstance(p, int) and p < len(self.first) else self.dst.at[p, me["z"]]
        src, dst = own.at[self.mine], self.dst.at[p, me["z"], self.mine]
        return remote(src, dst, self.ssem.at[p, k - 1], self.rsem.at[p, k - 1], me["w"], around(me, k))

    def x_copy(self, p, k):
        return self.along(p, k, self.mine, pl.ds(0, 1024), 3, self.me["wx"], self.me["z"], around(self.me, -k))

    def y_copy(self, p, k):
        return self.along(p, k, self.mine, pl.ds(0, 1024), 6, self.me["wy"], self.me["z"], around(self.me, -k))

    def xy_copy(self, p, k):
        return self.along(p, k, self.from_y, LEFT, 9, self.me["wx"], self.me["z"], around(self.me, -k))

    def yx_copy(self, p, k):
        return self.along(p, k, self.from_x, RIGHT, 12, self.me["wy"], self.me["z"], around(self.me, -k))

    def core_copy(self, p, k):
        return self.along(p, k, self.core_half, pl.ds(0, 1024), 15, self.me["wc"], self.me["z"], around(self.me, -k))

    def start_z(self, p):
        for k in range(1, ZN):
            self.z_copy(p, k).start()

    def stage_one(self, p):
        for k in range(1, ZN):
            self.z_copy(p, k).wait_recv()
            self.x_copy(p, k).start()
            self.y_copy(p, k).start()

    def stage_two(self, p):
        for k in range(1, ZN):
            self.y_copy(p, k).wait_recv()
            self.xy_copy(p, k).start()
            self.x_copy(p, k).wait_recv()
            self.yx_copy(p, k).start()

    def stage_core(self, p):
        for k in range(1, ZN):
            self.xy_copy(p, k).wait_recv()
            self.yx_copy(p, k).wait_recv()
            self.core_copy(p, k).start()

    def finish(self, p):
        for k in range(1, ZN):
            self.core_copy(p, k).wait_recv()
        for k in range(1, ZN):
            for copy in (self.z_copy, self.x_copy, self.y_copy, self.xy_copy, self.yx_copy, self.core_copy):
                copy(p, k).wait_send()


    def slot(self, t):
        n = self.dst.shape[0]
        for stage, lag in ((self.finish, 4), (self.stage_core, 3), (self.stage_two, 2), (self.stage_one, 1)):
            p = t - lag

            def due(stage=stage, p=p):
                stage(p)

            when((p >= 0) & (p < n), due)

        def begin():
            self.start_z(t)

        when((t >= len(self.first)) & (t < n), begin)


def add_up(*parts):
    total = parts[0].astype(F32)
    for one in parts[1:]:
        total = total + one.astype(F32)
    return total.astype(BF)


def when(cond, body):
    if isinstance(cond, bool):
        if cond:
            body()
    else:
        pl.when(cond)(body)


class Reduce:
    SCRATCH = [
        ((2, 4, 128, 1024), "g0"), ((2, 4, 128, 1024), "r0"), ((4, 128, 1024), "s0"), ((2, 2, 4, 64, 512), "r1"),
        ((2, 2, 2, 64, 512), "s1"), ((2, 2, 2, 64, 512), "r2"), ((2, 2, 64, 512), "s2"), ((2, 2, 64, 512), "r3"),
        ((2, 64, 512), "s3"), ((2, 2, 32, 512), "r4"), ((2, 2, 32, 512), "f"),
    ]
    LAST = 7

    def __init__(self, me, G, fin, bufs, ssem, rsem, lsem):
        self.me, self.G, self.fin, self.ssem, self.rsem, self.lsem = me, G, fin, ssem, rsem, lsem
        for (_shape, name), ref in zip(self.SCRATCH, bufs):
            setattr(self, name, ref)

    def to(self, p, i, src, dst, w, z=None):
        z = self.me["z"] if z is None else z
        slot = lax.rem(p, 2)
        return remote(src, dst, self.ssem.at[slot, i], self.rsem.at[slot, i], w, z)

    def copies(self, s, p):
        me = self.me
        a, b, c, slot = me["a"], me["b"], me["c"], lax.rem(p, 2)
        every = pl.ds(0, ZN)
        if s == 0:
            return [
                self.to(p, 0, self.G.at[p, every, part((1 - c) * 128, 128)], self.r0.at[slot], me["wc"]),
                pltpu.make_async_copy(self.G.at[p, every, part(c * 128, 128)], self.g0.at[slot], self.lsem.at[slot, 2]),
            ]
        if s == 1:
            return [
                self.to(p, 1, self.s0.at[every, part((1 - a) * 64, 64), LEFT], self.r1.at[slot, 0], me["wx"]),
                self.to(p, 2, self.s0.at[every, part((1 - b) * 64, 64), RIGHT], self.r1.at[slot, 1], me["wy"]),
            ]
        if s == 2:
            return [self.to(p, 3, self.s1.at[1 - me["lo"]], self.r2.at[slot], me["w"], me["zl"])]
        if s == 3:
            return [self.to(p, 4, self.s2.at[1 - me["hi"]], self.r3.at[slot], me["w"], me["zh"])]
        if s == 4:
            return [
                self.to(p, 5, self.s3.at[0, part((1 - b) * 32, 32)], self.r4.at[slot, 0], me["wy"]),
                self.to(p, 6, self.s3.at[1, part((1 - a) * 32, 32)], self.r4.at[slot, 1], me["wx"]),
            ]
        if s == 5:
            left = self.fin.at[p, part(c * 128 + a * 64 + b * 32, 32), LEFT]
            right = self.fin.at[p, part(c * 128 + b * 64 + a * 32, 32), RIGHT]
            return [
                self.to(p, 7, self.f.at[slot, 0], left, me["wy"]),
                self.to(p, 8, self.f.at[slot, 1], right, me["wx"]),
                pltpu.make_async_copy(self.f.at[slot, 0], left, self.lsem.at[slot, 0]),
                pltpu.make_async_copy(self.f.at[slot, 1], right, self.lsem.at[slot, 1]),
            ]
        if s == 6:
            left = self.fin.at[p, part(c * 128 + a * 64, 64), LEFT]
            right = self.fin.at[p, part(c * 128 + b * 64, 64), RIGHT]
            return [self.to(p, 9, left, left, me["wx"]), self.to(p, 10, right, right, me["wy"])]
        half = self.fin.at[p, part(c * 128, 128)]
        return [self.to(p, 11, half, half, me["wc"])]

    def start(self, s, p):
        for copy in self.copies(s, p):
            copy.start()

    def advance(self, s, p):
        for copy in self.copies(s, p):
            copy.wait()
        me = self.me
        a, b, slot = me["a"], me["b"], lax.rem(p, 2)
        if s == 0:
            for k in range(ZN):
                self.s0[k] = add_up(self.g0[slot, k], self.r0[slot, k])
        if s == 1:
            for k in range(ZN):
                self.s1[k % 2, 0, k // 2] = add_up(self.s0[k, part(a * 64, 64), 0:512], self.r1[slot, 0, k])
                self.s1[k % 2, 1, k // 2] = add_up(self.s0[k, part(b * 64, 64), 512:1024], self.r1[slot, 1, k])
        if s == 2:
            for hi in range(2):
                for side in range(2):
                    self.s2[hi, side] = add_up(self.s1[me["lo"], side, hi], self.r2[slot, side, hi])
        if s == 3:
            self.s3[...] = add_up(self.s2[me["hi"]], self.r3[slot])
        if s == 4:
            self.f[slot, 0] = add_up(self.s3[0, part(b * 32, 32), :], self.r4[slot, 0])
            self.f[slot, 1] = add_up(self.s3[1, part(a * 32, 32), :], self.r4[slot, 1])
        if s < self.LAST:
            self.start(s + 1, p)

    def slot(self, t, n):
        for s in range(self.LAST, -1, -1):
            p = t - 1 - s

            def due(s=s, p=p):
                self.advance(s, p)

            when((p >= 0) & (p < n), due)

        def begin():
            self.start(0, t)

        when(t < n, begin)


def loop(n, body):
    def step(i, _):
        body(i)
        return 0

    lax.fori_loop(0, n, step, 0)


def starts(make):
    def body(i):
        made = make(i)
        for copy in made if isinstance(made, list) else [made]:
            copy.start()

    return body


def waits(make):
    def body(i):
        made = make(i)
        for copy in made if isinstance(made, list) else [made]:
            copy.wait()

    return body


def attention_forward(i, pair, qaug, kaug, vaug, att):
    T = qaug.shape[0]
    low, high = max(0, i - 1) * BLK, min(T, (i + 2) * BLK)
    rows = slice(i * BLK, (i + 1) * BLK)
    outs, tops = [], []
    for one in range(2):
        cols = pl.ds(pl.multiple_of((2 * pair + one) * 128, 128), 128)
        scores = nt(qaug[rows, cols], kaug[low:high, cols])
        top = jnp.max(scores, axis=-1, keepdims=True)
        raised = jnp.exp2(scores - top).astype(BF)
        outs.append(nn(raised, vaug[low:high, cols]))
        tops.append(top)
    lane = lanes((BLK, 128))
    left = lane < HEAD
    for one in range(2):
        cols = pl.ds(pl.multiple_of((2 * pair + one) * 128, 128), 128)
        base = HEAD if one == 0 else 0
        parts = split_three(-(tops[one] + jnp.log2(outs[one])))
        kept = qaug[rows, cols].astype(F32)
        for k, term in enumerate(parts):
            kept = jnp.where(lane == base + 8 + k, term, kept)
        qaug[rows, cols] = kept.astype(BF)
    summed = pltpu.roll(jnp.where(left, outs[1], outs[0]), HEAD, axis=1)
    att[rows, pl.ds(pl.multiple_of(pair * 128, 128), 128)] = (
        jnp.where(left, outs[0], outs[1]) / summed
    ).astype(BF)


def project_turned(n1, W, cos, sin, aug, dest, scale):
    T = n1.shape[0]

    def block(j, _):
        flat = nn(n1[...], W[:, :, part(j * 256, 256)].reshape(n1.shape[1], 256))
        left = lanes((T, 128)) < HEAD
        for p in range(2):
            u = turn(flat[:, 128 * p : 128 * p + 128], cos[...], sin[...])
            if scale != 1.0:
                u = u * scale
            extra = aug[...].astype(F32)
            at = (4 * j + 2 * p) * 128
            dest[:, pl.ds(pl.multiple_of(at, 128), 128)] = jnp.where(left, u, extra).astype(BF)
            dest[:, pl.ds(pl.multiple_of(at + 128, 128), 128)] = jnp.where(left, extra, u).astype(BF)
        return 0

    lax.fori_loop(0, n1.shape[1] // 256, block, 0)


def project_values(n1, W, dest):
    T = n1.shape[0]

    def block(j, _):
        flat = nn(n1[...], W[:, :, part(j * 256, 256)].reshape(n1.shape[1], 256))
        left = lanes((T, 128)) < HEAD
        for p in range(2):
            u = flat[:, 128 * p : 128 * p + 128]
            at = (4 * j + 2 * p) * 128
            dest[:, pl.ds(pl.multiple_of(at, 128), 128)] = jnp.where(left, u, 1.0).astype(BF)
            dest[:, pl.ds(pl.multiple_of(at + 128, 128), 128)] = jnp.where(left, 1.0, u).astype(BF)
        return 0

    lax.fori_loop(0, n1.shape[1] // 256, block, 0)


def norm_rows(source, dest, gain, bias, n=BLK):
    def block(r, _):
        rows = pl.ds(pl.multiple_of(r * n, n), n)
        hat, _unused = hat_of(source[rows, :].astype(F32))
        dest[rows, :] = (hat * gain + bias).astype(BF)
        return 0

    lax.fori_loop(0, source.shape[0] // n, block, 0)


def feed_values(n2, cot, gate_up, down, hid, dgu):
    D = n2.shape[1]
    half = hid.shape[1]
    gu = nn(n2[...], gate_up[...].reshape(D, 2 * half))
    g = gu[:, :half]
    u = gu[:, half:]
    gh = nt(cot[...], down[...].reshape(half, D))
    sig = 0.5 * jnp.tanh(0.5 * g) + 0.5
    silu = g * sig
    hid[...] = (silu * u).astype(BF)
    dgu[:, :half] = (gh * u * (sig + silu * (1.0 - sig))).astype(BF)
    dgu[:, half:] = (gh * silu).astype(BF)


def feed_sums(gate_up, down, hid, dgu, oacc, gacc):
    half, D = hid.shape[1], dgu.shape[1]
    oacc[...] += nn(hid[...], down[...].reshape(half, D))
    gacc[...] += nt(dgu[...], gate_up[...].reshape(D, 2 * half))


def feed_finish(gacc, mixed, cot, vec, vecs):
    def block(r, _):
        rows = pl.ds(pl.multiple_of(r * BLK, BLK), BLK)
        hat, rstd = hat_of(mixed[rows, :])
        grad = gacc[rows, :]
        vecs[2:3, :] += jnp.sum(grad * hat, axis=0, keepdims=True)
        vecs[3:4, :] += jnp.sum(grad, axis=0, keepdims=True)
        mixed[rows, :] = cot[rows, :].astype(F32) + norm_back(grad, hat, rstd, vec[2:3, :])
        return 0

    lax.fori_loop(0, mixed.shape[0] // BLK, block, 0)


def attention_backward(j, pair, qaug, kaug, vaug, doaug, dq, dk, dv):
    T = qaug.shape[0]
    low, high = max(0, j - 1) * BLK, min(T, (j + 2) * BLK)
    keys = slice(j * BLK, (j + 1) * BLK)
    sums = []
    for one in range(2):
        cols = pl.ds(pl.multiple_of((2 * pair + one) * 128, 128), 128)
        prob = jnp.exp2(nt(kaug[keys, cols], qaug[low:high, cols]))
        grad = nt(vaug[keys, cols], doaug[low:high, cols])
        prob_low = prob.astype(BF)
        gs = (prob * grad).astype(BF)
        sums.append((
            nn(prob_low, doaug[low:high, cols]),
            nn(gs, qaug[low:high, cols]),
            tn(gs, kaug[keys, cols]),
        ))
    left = lanes((BLK, 128)) < HEAD
    dv[keys, :] = jnp.where(left, sums[0][0], sums[1][0])
    dk[keys, :] = jnp.where(left, sums[0][1], sums[1][1]) * (1.0 / LOG2E)
    left = lanes((high - low, 128)) < HEAD
    dq[low:high, :] += jnp.where(left, sums[0][2], sums[1][2]) * (1.0 / math.sqrt(HEAD))


def head_grads(grad_res, att, W, doaug):
    T, D = grad_res.shape

    def block(j, _):
        flat = nt(grad_res[...], W[j])
        lane = lanes((T, 128))
        left = lane < HEAD
        for p in range(2):
            grad = flat[:, 128 * p : 128 * p + 128].astype(BF).astype(F32)
            prod = grad * att[:, :, part(j * 256 + 128 * p, 128)].reshape(T, 128).astype(F32)
            for one in range(2):
                own = left if one == 0 else lane >= HEAD
                dot = jnp.sum(jnp.where(own, prod, 0.0), axis=-1, keepdims=True)
                base = HEAD if one == 0 else 0
                kept = jnp.where(own, grad, 0.0)
                for k, term in enumerate(split_three(-dot)):
                    kept = jnp.where(lane == base + 8 + k, term, kept)
                at = (4 * j + 2 * p + one) * 128
                doaug[:, pl.ds(pl.multiple_of(at, 128), 128)] = kept.astype(BF)
        return 0

    lax.fori_loop(0, D // 256, block, 0)


def backward_pair(pair, qaug, kaug, vaug, doaug, dq, dk, dv, cos, sin, dqkv):
    T = qaug.shape[0]
    dq[...] = jnp.zeros_like(dq)
    for j in range(T // BLK):
        attention_backward(j, pair, qaug, kaug, vaug, doaug, dq, dk, dv)
    cols = pl.ds(pl.multiple_of(pair * 128, 128), 128)
    dqkv[0][:, cols] = unturn(dq[...], cos[...], sin[...]).astype(BF)
    dqkv[1][:, cols] = unturn(dk[...], cos[...], sin[...]).astype(BF)
    dqkv[2][:, cols] = dv[...].astype(BF)


def input_finish(gn1, x, gm, vec, vecs):
    def rows_of(r, _):
        rows = pl.ds(pl.multiple_of(r * BLK, BLK), BLK)
        hat, rstd = hat_of(x[rows, :].astype(F32))
        grad = gn1[rows, :]
        vecs[0:1, :] += jnp.sum(grad * hat, axis=0, keepdims=True)
        vecs[1:2, :] += jnp.sum(grad, axis=0, keepdims=True)
        gm[rows, :] += norm_back(grad, hat, rstd, vec[0:1, :])
        return 0

    lax.fori_loop(0, x.shape[0] // BLK, rows_of, 0)


def tables(lengths, inverse, cos, sin, aq, ak):
    shape = cos.shape
    places = lax.broadcasted_iota(jnp.int32, shape, 0)
    segment = jnp.zeros(shape, jnp.int32)
    offset = jnp.zeros(shape, jnp.int32)
    end = jnp.int32(0)
    for j in range(lengths.shape[1]):
        end = end + lengths[0, j]
        before = places >= end
        segment = segment + jnp.where(before, 1, 0)
        offset = jnp.where(before, end, offset)
    angles = (places - offset).astype(F32) * inverse[0:1, :]
    place = lax.rem(lanes(shape), HEAD)
    cos[...] = jnp.cos(angles)
    sines = jnp.sin(angles)
    sin[...] = jnp.where(place < HEAD // 2, -sines, sines)
    mine = segment == place
    aq[...] = jnp.where(mine, 1.0, 0.0).astype(BF)
    other = jnp.where(mine, 0.0, -1e30)
    ak[...] = jnp.where(place < 8, other, jnp.where(place < 11, 1.0, 0.0)).astype(BF)


CHUNKS = 8


def kernel_layer(
    tok_h, cot_h, vec_h, lengths, inverse, wq_h, wk_h, wv_h, wo_h, gate_h, up_h, down_h,
    out_h, ig_h, vsum_h, fin_h, dst, G_h, n1_h, att_h, mixed_h,
    F0, F1, Q, K, V, DO, PB, b0, b1, b2, GO, GD, dq, dk, dv, cos, sin, aq, ak, vec, vecs, vgot, *rest,
):
    bufs, (lsem, fsem, wsem, gsem, gssem, grsem, rssem, rrsem, rlsem, vssem, vrsem) = rest[:11], rest[11:]
    T, D = b0.shape
    me = place()
    z = me["z"]
    used = [0]

    def cp(src, dst_ref):
        copy = pltpu.make_async_copy(src, dst_ref, lsem.at[used[0]])
        used[0] += 1
        copy.start()
        return copy

    own_weights = (wq_h, wk_h, wv_h, wo_h)
    c_vec = cp(vec_h, vec.at[:, part(z * 256, 256)])
    c_tok = cp(tok_h, b0)
    c_own = [cp(own_weights[i], PB.at[i, z]) for i in range(4)]
    c_down = cp(down_h, b1)

    def feed_in(i):
        made = []
        rows = part(256 * lax.rem(i, 4), 256)
        for j in range(ZN):
            cols = part(1024 * j + 128 * i, 128)
            for k, source in enumerate((gate_h, up_h)):
                to = part(1024 * (i // 4) + 512 * k + 128 * j, 128)
                made.append(pltpu.make_async_copy(source.at[:, cols], DO.at[rows, to], fsem.at[i, 2 * j + k]))
        return made

    def feed_out(i):
        at = 4 + 3 * (i // 2) + lax.rem(i, 2)
        source = DO.at[part(256 * lax.rem(i, 4), 256), part(1024 * (i // 4), 1024)]
        return pltpu.make_async_copy(source, dst.at[at, z], fsem.at[i, 0])

    def down_out(i):
        return pltpu.make_async_copy(b1.at[part(256 * i, 256)], dst.at[6 + 3 * i, z], fsem.at[i, 1])

    loop(CHUNKS, starts(feed_in))
    meet(me)
    g = Gather(me, own_weights, dst, gssem, grsem)
    r = Reduce(me, G_h, fin_h, bufs, rssem, rrsem, rlsem)

    def vec_copy(k):
        return remote(vec_h, vec.at[:, part(z * 256, 256)], vssem.at[k - 1], vrsem.at[k - 1], me["w"], around(me, k))

    for k in range(1, ZN):
        vec_copy(k).start()
    for p in range(4):
        g.start_z(p)
    loop(CHUNKS, waits(feed_in))
    loop(CHUNKS, starts(feed_out))
    c_down.wait()
    loop(4, starts(down_out))
    c_own_out = []
    for i in range(4):
        c_own[i].wait()
        c_own_out.append(cp(PB.at[i, z], dst.at[i, z]))
    c_tok.wait()
    c_vec.wait()
    for k in range(1, ZN):
        vec_copy(k).wait()
    norm_rows(b0, b2, vec[0:1, :], vec[1:2, :])
    c_n1 = [cp(b2.at[pl.ds(256 * k, 256)], n1_h.at[k]) for k in range(ZN)]
    tables(lengths, inverse, cos, sin, aq, ak)

    def bring(p):
        return [cp(dst.at[p, around(me, k)], PB.at[p, around(me, k)]) for k in range(1, ZN)]

    g.slot(1)
    g.slot(2)
    g.slot(3)
    loop(CHUNKS, waits(feed_out))
    loop(4, waits(down_out))
    g.slot(4)
    for one in bring(0):
        one.wait()
    project_turned(b2, PB.at[0], cos, sin, aq, Q, LOG2E / math.sqrt(HEAD))
    g.slot(5)
    for one in bring(1):
        one.wait()
    project_turned(b2, PB.at[1], cos, sin, ak, K, 1.0)
    g.slot(6)
    for one in bring(2):
        one.wait()
    project_values(b2, PB.at[2], V)
    g.slot(7)
    c_out_weight = bring(3)

    def pair_forward(pair, _):
        for i in range(T // BLK):
            attention_forward(i, pair, Q, K, V, b1)

        @pl.when(lax.rem(pair, 2) == 1)
        def _gather():
            g.slot(8 + pair // 2)

        return 0

    lax.fori_loop(0, D // 128, pair_forward, 0)
    c_att = [cp(b1.at[pl.ds(256 * k, 256)], att_h.at[k]) for k in range(ZN)]
    for one in c_out_weight + c_own_out + c_n1:
        one.wait()
    F0[...] = b0[...].astype(F32) + nn(b1[...], PB[3].reshape(D, D))

    def load(c):
        at, slot = 4 + 3 * (c // 2), lax.rem(c, 2)
        return pltpu.make_async_copy(dst.at[at + slot], PB.at[slot], wsem.at[slot])

    def load_down(c):
        slot = lax.rem(c // 2, 2)
        return pltpu.make_async_copy(dst.at[6 + 3 * (c // 2)], PB.at[2 + slot], wsem.at[2 + slot])

    load(jnp.int32(0)).start()
    load_down(jnp.int32(0)).start()
    c_mixed = cp(F0, mixed_h)
    c_cot = cp(cot_h, b0)
    g.slot(12)
    norm_rows(F0, b2, vec[2:3, :], vec[3:4, :])
    for one in c_att + [c_mixed, c_cot]:
        one.wait()
    F1[...] = jnp.zeros_like(F1)
    hid, dgu = DO.at[:, pl.ds(D, D // 2)], DO.at[:, pl.ds(0, D)]

    def stored(c):
        at, slot = 3 * (c // 2), lax.rem(c, 2)
        return [
            pltpu.make_async_copy(GO, G_h.at[at + slot], gsem.at[0]),
            pltpu.make_async_copy(GD, G_h.at[at + 2, :, part(slot * 128, 128)], gsem.at[1]),
        ]

    def chunk(c, _):
        slot = lax.rem(c, 2)
        load(c).wait()

        @pl.when(slot == 0)
        def _down():
            load_down(c).wait()

        @pl.when(c < CHUNKS - 1)
        def _next():
            load(c + 1).start()

        @pl.when((c < CHUNKS - 1) & (slot == 1))
        def _next_down():
            load_down(c + 1).start()

        gate_up = PB.at[slot]
        down = PB.at[2 + lax.rem(c // 2, 2), :, part(slot * 128, 128)]
        feed_values(b2, b0, gate_up, down, hid, dgu)
        g.slot(13 + 2 * c)
        feed_sums(gate_up, down, hid, dgu, F0, F1)

        @pl.when(c >= 1)
        def _sums():
            waits(stored)(c - 1)
            r.slot(c - 1, 16)

        GO[...] = tn(b2[...], dgu[...]).astype(BF).reshape(GO.shape)
        GD[...] = tn(hid[...], b0[...]).astype(BF).reshape(GD.shape)
        starts(stored)(c)
        g.slot(14 + 2 * c)
        return 0

    lax.fori_loop(0, CHUNKS, chunk, 0)

    def whole(source, slot):
        return cp(source, PB.at[slot])

    c_wo = whole(dst.at[3], 2)
    c_att = whole(att_h, 0)
    c_n1 = whole(n1_h, 1)
    b1[...] = F0[...].astype(BF)
    c_out = cp(b1, out_h)
    c_mixed = cp(mixed_h, F0)
    waits(stored)(CHUNKS - 1)
    r.slot(jnp.int32(7), 16)
    c_mixed.wait()
    vecs[...] = jnp.zeros_like(vecs)
    feed_finish(F1, F0, b0, vec, vecs)
    b2[...] = F0[...].astype(BF)

    c_wo.wait()
    c_att.wait()
    head_grads(b2, PB.at[0], PB.at[2], DO)
    GO[...] = tn(PB[0].reshape(T, D), b2[...]).astype(BF).reshape(GO.shape)
    c_go = cp(GO, G_h.at[12])
    c_wq = whole(dst.at[0], 3)
    c_wk = whole(dst.at[1], 0)
    c_wv = whole(dst.at[2], 2)
    r.slot(jnp.int32(8), 16)
    c_go.wait()
    c_out.wait()

    def pair_backward(pair, _):
        backward_pair(pair, Q, K, V, DO, dq, dk, dv, cos, sin, (b0, b1, b2))

        @pl.when(lax.rem(pair, 2) == 1)
        def _sums():
            r.slot(9 + pair // 2, 16)

        return 0

    lax.fori_loop(0, D // 128, pair_backward, 0)
    c_n1.wait()
    for k, (grad, weight, at) in enumerate(((b0, c_wq, 3), (b1, c_wk, 0), (b2, c_wv, 2))):
        GO[...] = tn(PB[1].reshape(T, D), grad[...]).astype(BF).reshape(GO.shape)
        c_go = cp(GO, G_h.at[13 + k])
        weight.wait()
        term = nt(grad[...], PB[at].reshape(D, D))
        F1[...] = term if k == 0 else F1[...] + term
        c_go.wait()
        r.slot(jnp.int32(13 + k), 16)
        if k == 0:
            c_tok = cp(tok_h, b0)
    c_tok.wait()
    r.slot(jnp.int32(16), 16)
    input_finish(F1, b0, F0, vec, vecs)
    c_ig = cp(F0, ig_h)

    steps = [(me["wc"], z), (me["wx"], z), (me["wy"], z), (me["w"], me["zl"]), (me["w"], me["zh"])]

    def vec_step(i):
        return remote(vecs, vgot.at[i], vssem.at[3 + i], vrsem.at[3 + i], steps[i][0], steps[i][1])

    vec_step(0).start()
    for t in range(17, 24):
        i = t - 17
        if i < 5:
            vec_step(i).wait()
            vecs[...] += vgot[i]
            if i < 4:
                vec_step(i + 1).start()
        r.slot(jnp.int32(t), 16)
    c_vs = cp(vecs, vsum_h)
    c_vs.wait()
    c_ig.wait()


def run_layer(tok, cot, vec, lengths, inverse, *weights):
    T, D = tok.shape
    sds, v, sem = jax.ShapeDtypeStruct, pltpu.VMEM, pltpu.SemaphoreType.DMA
    piece = (ZN, 256, D)
    return pl.pallas_call(
        kernel_layer,
        name="layer",
        out_shape=[
            sds((T, D), BF), sds((T, D), F32), sds((8, D), F32), sds((16, 256, D), BF), sds((16,) + piece, BF),
            sds((16,) + piece, BF), sds(piece, BF), sds(piece, BF), sds((T, D), F32),
        ],
        in_specs=[ANY] * 3
        + [pl.BlockSpec(memory_space=pltpu.SMEM), pl.BlockSpec(memory_space=pltpu.VMEM)]
        + [ANY] * 7,
        out_specs=[ANY] * 9,
        scratch_shapes=[
            v((T, D), F32), v((T, D), F32), v((T, 2 * D), BF), v((T, 2 * D), BF), v((T, 2 * D), BF), v((T, 2 * D), BF),
            v((4,) + piece, BF), v((T, D), BF), v((T, D), BF), v((T, D), BF), v(piece, BF), v((ZN, 128, D), BF),
            v((T, 128), F32), v((T, 128), F32), v((T, 128), F32), v((T, 128), F32), v((T, 128), F32),
            v((T, 128), BF), v((T, 128), BF), v((8, D), F32), v((8, D), F32), v((5, 8, D), F32),
        ]
        + [v(shape, BF) for shape, _ in Reduce.SCRATCH]
        + [
            sem((64,)), sem((8, 8)), sem((4,)), sem((2,)), sem((16, 18)), sem((16, 18)),
            sem((2, 12)), sem((2, 12)), sem((2, 3)), sem((8,)), sem((8,)),
        ],
        compiler_params=pltpu.CompilerParams(collective_id=0, has_side_effects=True, vmem_limit_bytes=63 * MIB),
    )(tok, cot, vec, lengths, inverse, *weights)


def kernel_spread(fin_h, q_h, k_h, v_h, o_h, gate_h, up_h, down_h, fin, wide, sems, osems):
    n = fin_h.shape[0]
    load = [pltpu.make_async_copy(fin_h.at[p], fin.at[p], sems.at[p]) for p in range(n)]
    for copy in load:
        copy.start()
    out = []
    for p in range(n):
        load[p].wait()
        wide[p] = fin[p].astype(F32)
        made = []
        if p >= 12:
            made.append((wide.at[p], (o_h, q_h, k_h, v_h)[p - 12]))
        elif p % 3 == 2:
            made.append((wide.at[p], down_h.at[pl.ds(256 * (p // 3), 256)]))
        else:
            i = 2 * (p // 3) + p % 3
            for j in range(ZN):
                cols = pl.ds(1024 * j + 128 * i, 128)
                made.append((wide.at[p, :, pl.ds(128 * j, 128)], gate_h.at[:, cols]))
                made.append((wide.at[p, :, pl.ds(512 + 128 * j, 128)], up_h.at[:, cols]))
        out += [pltpu.make_async_copy(x, y, osems.at[p, i]) for i, (x, y) in enumerate(made)]
        for copy in out[-len(made) :]:
            copy.start()
    for copy in out:
        copy.wait()


def run_spread(fin, shapes):
    return pl.pallas_call(
        kernel_spread,
        name="spread_sums",
        out_shape=[jax.ShapeDtypeStruct(shape, F32) for shape in shapes],
        in_specs=[ANY],
        out_specs=[ANY] * len(shapes),
        scratch_shapes=[
            pltpu.VMEM(fin.shape, BF), pltpu.VMEM(fin.shape, F32),
            pltpu.SemaphoreType.DMA((16,)), pltpu.SemaphoreType.DMA((16, 8)),
        ],
        compiler_params=pltpu.CompilerParams(vmem_limit_bytes=40 * MIB),
    )(fin)


def sum_rest(part_sum):
    size, step = lax.axis_size("wide"), 8
    while step < size:
        pairs = [(i, (i // (2 * step)) * 2 * step + (i + step) % (2 * step)) for i in range(size)]
        other = lax.ppermute(part_sum, "wide", pairs)
        part_sum = (part_sum.astype(F32) + other.astype(F32)).astype(part_sum.dtype)
        step *= 2
    return part_sum


def shards(
    tokens, lengths, ln1_gain, ln1_bias, w_query, w_key, w_value, w_out,
    ln2_gain, ln2_bias, w_gate, w_up, w_down, cotangent,
):
    _rows, T, D = tokens.shape
    DR = D // ZN
    vec = jnp.stack([v.astype(F32) for v in (ln1_gain, ln1_bias, ln2_gain, ln2_bias)])
    vec = jnp.concatenate([vec, jnp.zeros_like(vec)])
    power = np.tile(np.arange(HEAD // 2, dtype=np.float32), 4) * np.float32(-2.0 / HEAD)
    inverse = jnp.asarray(np.tile(np.power(np.float32(ROTARY_BASE), power)[None], (8, 1)).astype(np.float32))
    weights = (w_query, w_key, w_value, w_out, w_gate, w_up, w_down)
    out, input_grad, vsum, fin = run_layer(tokens[0], cotangent[0], vec, lengths, inverse, *weights)[:4]
    sums = run_spread(sum_rest(fin), [w.shape for w in weights])
    mine = lax.dynamic_slice_in_dim(sum_rest(vsum), lax.axis_index("narrow") * DR, DR, axis=1)
    return (out[None], input_grad[None], mine[0], mine[1], *sums[:4], mine[2], mine[3], *sums[4:])


def solution(mesh):
    both = ("wide", "narrow")
    row3, row2, vector, matrix = P(both, None, None), P(both, None), P("narrow"), P("narrow", None)
    weights = (vector, vector, matrix, matrix, matrix, matrix, vector, vector, matrix, matrix, matrix)
    return jax.shard_map(
        shards,
        mesh=mesh,
        in_specs=(row3, row2) + weights + (row3,),
        out_specs=(row3, row3) + weights,
        check_vma=False,
    )
```
